256 devices in a mesh: blk: 64 (over x_lo, z, y), rep: 4 (over x_hi, core).
Axes of the slice: x: 4 (x_hi: 2, x_lo: 2; x = x_hi * 2 + x_lo), y: 4, z: 8, core: 2. Of those that a mesh axis runs over, the one named last changes fastest.
Arguments:
- image: bfloat16 [4, 8192, 1536], P('rep', 'blk'), may hold values from -8 to 8
- text: bfloat16 [4, 8192, 1536], P('rep', 'blk'), may hold values from -8 to 8
- log_scale: float32 [], replicated, may hold values from 2.3 to 3
- bias: float32 [], replicated, may hold values from -4 to -1
- head: bfloat16 [1536, 768], replicated, may hold values from -0.15625 to 0.15625
Outputs:
- loss: float32 [], replicated
- scale_grad: float32 [], replicated
- bias_grad: float32 [], replicated
- image_grad: bfloat16 [4, 8192, 1536], P('rep', 'blk')
- text_grad: bfloat16 [4, 8192, 1536], P('rep', 'blk')
- head_grad: float32 [1536, 768], P('blk')
The draws below stay inside these ranges and needn't reach their ends.
All inputs are finite; a program needn't handle non-finite values.
Results may differ from the reference program's by a relative error of at most 0.0095.
Values may be sent and summed in bfloat16 or wider, within the bound.
No kernel may reach another device: no remote copies, remote signals or barrier semaphores. Data moves between devices by JAX's collectives and lax.ppermute only.
A program may use at most 128 MiB of HBM per device.

```python
import math
import jax
import jax.numpy as jnp
from jax import lax

D = 1536
E = 768
PAIRS = 8192
REPLICAS = 4


def pick_rows(table, index_rows):
    return table[index_rows]


def shared_parts(key):
    class_ids = jax.random.randint(jax.random.fold_in(key, 11), (REPLICAS, PAIRS), 0, 32)
    centers = jax.random.normal(jax.random.fold_in(key, 12), (REPLICAS, 32, D), jnp.float32)
    picked = jax.vmap(pick_rows)(centers, class_ids)
    shared = jax.random.normal(jax.random.fold_in(key, 13), (REPLICAS, PAIRS, D), jnp.float32)
    return (picked, shared)


def position_ramp(key, power):
    place = (jnp.arange(PAIRS, dtype=jnp.float32) + 0.5) / float(PAIRS)
    jitter = jax.random.uniform(key, (REPLICAS, PAIRS, 1), jnp.float32, 0.7, 1.3)
    return 3.6 * (place ** power)[None, :, None] * jitter


def draw_image(key, part):
    picked, shared = shared_parts(key)
    key = jax.random.fold_in(key, 1)
    strength = position_ramp(jax.random.fold_in(key, 2), 1.0)
    values = strength * picked + shared
    return jnp.clip(values, -8.0, 8.0).astype(jnp.bfloat16)


def draw_text(key, part):
    picked, shared = shared_parts(key)
    key = jax.random.fold_in(key, 2)
    mixing = jax.random.uniform(jax.random.fold_in(key, 4), (REPLICAS, PAIRS, 1), jnp.float32, 0.0, 1.2)
    fresh = jax.random.normal(jax.random.fold_in(key, 5), (REPLICAS, PAIRS, D), jnp.float32)
    strength = position_ramp(jax.random.fold_in(key, 2), 1.0)
    values = strength * picked + mixing * shared + fresh
    return jnp.clip(values, -8.0, 8.0).astype(jnp.bfloat16)


def scatter_about(key, dims, deviation, reach, held_as=jnp.bfloat16):
    entries = jax.random.normal(key, dims, jnp.float32) * deviation
    return jnp.minimum(jnp.maximum(entries, -reach), reach).astype(held_as)


def setup_inputs(seed: int = 0) -> dict:
    key_list = jax.random.split(jax.random.key(seed), 6)
    return {
        "image": draw_image(jax.random.fold_in(key_list[5], 71), 0),
        "text": draw_text(jax.random.fold_in(key_list[5], 71), 0),
        "log_scale": jnp.clip(jax.random.uniform(key_list[2], (), jnp.float32, 2.3, 3.0), 2.3, 3.0),
        "bias": jnp.clip(jax.random.uniform(key_list[3], (), jnp.float32, -4.0, -1.0), -4.0, -1.0),
        "head": scatter_about(key_list[4], (D, E), D ** -0.5, 0.15625),
    }


def pass_blocks(rows_b, cols_b, scale, bias):
    count = rows_b.shape[0]
    step = math.gcd(count, 512)
    blocks = rows_b.reshape(count // step, step, rows_b.shape[1])
    starts = jnp.arange(count // step, dtype=jnp.int32) * step
    col_ids = jnp.arange(cols_b.shape[0], dtype=jnp.int32)

    def one_block(item):
        block, start = item
        sims = jnp.dot(block, cols_b.T, preferred_element_type=jnp.float32)
        logits = scale * sims + bias
        row_ids = start + jnp.arange(step, dtype=jnp.int32)
        sign = 2.0 * (row_ids[:, None] == col_ids[None, :]).astype(jnp.float32) - 1.0
        grads = -sign * jax.nn.sigmoid(-sign * logits)
        acc = jnp.dot(grads.astype(jnp.bfloat16), cols_b, preferred_element_type=jnp.float32)
        return (acc, jnp.sum(jax.nn.softplus(-sign * logits)), jnp.sum(grads * sims), jnp.sum(grads))
    acc, lsum, ssum, bsum = lax.map(one_block, (blocks, starts))
    return (acc.reshape(count, cols_b.shape[1]), jnp.sum(lsum), jnp.sum(ssum), jnp.sum(bsum))

def project(data, head):
    proj = jnp.dot(data, head, preferred_element_type=jnp.float32)
    norm = jnp.sqrt(lax.optimization_barrier(jnp.sum(proj * proj, axis=1, keepdims=True)) + 1e-06)
    return (proj / norm, norm)

def backnorm(unit, norm, grad):
    return (grad - unit * lax.optimization_barrier(jnp.sum(unit * grad, axis=1, keepdims=True))) / norm

def reference(image, text, log_scale, bias, head):
    scale = jnp.exp(log_scale)
    head_total = jnp.zeros(head.shape, jnp.float32)
    total_l = jnp.float32(0.0)
    total_s = jnp.float32(0.0)
    total_b = jnp.float32(0.0)
    image_out = []
    text_out = []
    for index in range(REPLICAS):
        xdata = image[index]
        ydata = text[index]
        unit_img, norm_img = project(xdata, head)
        unit_txt, norm_txt = project(ydata, head)
        u_b = unit_img.astype(jnp.bfloat16)
        v_b = unit_txt.astype(jnp.bfloat16)
        du, lsum, ssum, bsum = pass_blocks(u_b, v_b, scale, bias)
        dv, unused_l, unused_s, unused_b = pass_blocks(v_b, u_b, scale, bias)
        total_l = total_l + lsum
        total_s = total_s + ssum
        total_b = total_b + bsum
        dimg_b = backnorm(unit_img, norm_img, scale * du).astype(jnp.bfloat16)
        dtxt_b = backnorm(unit_txt, norm_txt, scale * dv).astype(jnp.bfloat16)
        image_out.append(jnp.dot(dimg_b, head.T, preferred_element_type=jnp.float32).astype(jnp.bfloat16))
        text_out.append(jnp.dot(dtxt_b, head.T, preferred_element_type=jnp.float32).astype(jnp.bfloat16))
        head_total = head_total + jnp.dot(xdata.T, dimg_b, preferred_element_type=jnp.float32) + jnp.dot(ydata.T, dtxt_b, preferred_element_type=jnp.float32)
    count = float(PAIRS) * float(PAIRS) * float(REPLICAS)
    return (total_l / count, scale * total_s / count, total_b / count, jnp.stack(image_out), jnp.stack(text_out), head_total)
```

```python
import functools

import jax
import jax.numpy as jnp
from jax import lax
from jax.experimental import pallas as pl
from jax.experimental.pallas import tpu as pltpu
from jax.sharding import Mesh, PartitionSpec as P

F32 = jnp.float32
BF16 = jnp.bfloat16
LOG2E = 1.4426950408889634
LN2 = 0.6931471805599453
VMEM_LIMIT = 50 * 1024 * 1024
R = 128
E = 768
D = 1536
H = E // 2

NT = (((1,), (1,)), ((), ()))
NN = (((1,), (0,)), ((), ()))
TN = (((0,), (0,)), ((), ()))


def dot(a, b, dims):
    return lax.dot_general(a, b, dims, preferred_element_type=F32)


def vmem_call(kernel, out_shape, scratch=(), smem_first=False, n_in=0, flops=0, nbytes=0):
    specs = [pl.BlockSpec(memory_space=pltpu.VMEM)] * n_in
    if smem_first:
        specs[0] = pl.BlockSpec(memory_space=pltpu.SMEM)
    return pl.pallas_call(
        kernel,
        out_shape=out_shape,
        in_specs=specs,
        out_specs=jax.tree.map(lambda _: pl.BlockSpec(memory_space=pltpu.VMEM), out_shape),
        scratch_shapes=list(scratch),
        compiler_params=pltpu.CompilerParams(vmem_limit_bytes=VMEM_LIMIT),
        cost_estimate=pl.CostEstimate(flops=flops, bytes_accessed=nbytes, transcendentals=0),
    )


def proj_kernel(x_ref, y_ref, head_ref, ui_ref, ni_ref, ub_ref, ut_ref, nt_ref, vb_ref):
    head = head_ref[...]
    for src, unit_ref, norm_ref, b_ref in (
        (y_ref, ut_ref, nt_ref, vb_ref),
        (x_ref, ui_ref, ni_ref, ub_ref),
    ):
        proj = dot(src[...], head, NN)
        norm = jnp.sqrt(jnp.sum(proj * proj, axis=1, keepdims=True) + 1e-06)
        unit = proj / norm
        unit_ref[...] = unit
        norm_ref[...] = norm
        b_ref[...] = unit.astype(BF16)


def project(x, y, head):
    unit = jax.ShapeDtypeStruct((R, E), F32)
    norm = jax.ShapeDtypeStruct((R, 1), F32)
    low = jax.ShapeDtypeStruct((R, E), BF16)
    return vmem_call(
        proj_kernel, (unit, norm, low, unit, norm, low), n_in=3,
        flops=4 * R * D * E, nbytes=2 * (2 * R * D + D * E),
    )(x, y, head)


SUB = 8
CB = 256
RB = 32


def pair_elementwise(s_ref, g_ref, rows, scale2, bias2, own):
    acc_m = jnp.zeros((SUB, CB), F32)
    acc_l = jnp.zeros((SUB, CB), F32)
    acc_s = jnp.zeros((SUB, CB), F32)
    acc_g = jnp.zeros((SUB, CB), F32)

    def fold(t):
        return jnp.sum(t.reshape(RB // SUB, SUB, CB), axis=0)

    for c in range(s_ref.shape[1] // CB):
        prod = jnp.ones((SUB, CB), F32)
        for r in range(rows // RB):
            s = s_ref[r * RB : (r + 1) * RB, c * CB : (c + 1) * CB]
            z = s * scale2 + bias2
            diag = own and c * CB < R
            if diag:
                row = r * RB + lax.broadcasted_iota(jnp.int32, (RB, CB), 0)
                col = c * CB + lax.broadcasted_iota(jnp.int32, (RB, CB), 1)
                mask = row == col
                z = jnp.where(mask, -z, z)
            t = jnp.exp2(-jnp.abs(z))
            one_t = 1.0 + t
            inv = 1.0 / one_t
            g = jnp.where(z >= 0.0, inv, t * inv)
            if diag:
                g = jnp.where(mask, -g, g)
            g_ref[r * RB : (r + 1) * RB, c * CB : (c + 1) * CB] = g.astype(BF16)
            acc_m = acc_m + fold(jnp.maximum(z, 0.0))
            acc_s = acc_s + fold(g * s)
            acc_g = acc_g + fold(g)
            for k in range(RB // SUB):
                prod = prod * one_t[k * SUB : (k + 1) * SUB]
        acc_l = acc_l + jnp.log(prod)
    return LN2 * acc_m + acc_l, acc_s, acc_g


def pair_kernel(chunks, first, scal_ref, *refs):
    n = sum(chunks)
    u_refs, refs = refs[:n], refs[n:]
    v_refs, refs = refs[:6], refs[6:]
    if first:
        du_ref, dv_ref, sums_ref, v_all, u_all, g_all, s_all = refs
    else:
        dv_in, du_ref, near_ref, far_ref, sums_ref, v_all, u_all, g_all, s_all = refs
    scale2 = scal_ref[0, 0]
    bias2 = scal_ref[0, 1]
    at = 0
    for ref in v_refs:
        v_all[at : at + ref.shape[0]] = ref[...]
        at += ref.shape[0]
    for i, ref in enumerate(u_refs):
        u_all[i * R : (i + 1) * R] = ref[...]
    v = v_all[...]
    tot = None
    at = 0
    for i, units in enumerate(chunks):
        rows = units * R
        s_all[i % 2, :rows] = dot(u_all[at : at + rows], v, NT)
        part = pair_elementwise(
            s_all.at[i % 2], g_all.at[pl.ds(at, rows)], rows, scale2, bias2, first and i == 0
        )
        tot = part if tot is None else tuple(a + b for a, b in zip(tot, part))
        du_ref[at : at + rows] = dot(g_all[at : at + rows], v, NN).astype(du_ref.dtype)
        at += rows
    dv = dot(g_all[...], u_all[...], TN)
    if first:
        dv_ref[...] = dv
    else:
        dv = dv + dv_in[...]
        near_ref[...] = dv[:E]
        far_ref[...] = dv[E:].astype(BF16)
    for i in range(3):
        sums_ref[i] = tot[i]


def pair(chunks, first, scal, us, vs, dv_in=None):
    n = sum(chunks)
    cols = 8 * R
    sums = jax.ShapeDtypeStruct((3, SUB, CB), F32)
    if first:
        out = (jax.ShapeDtypeStruct((n * R, E), F32), jax.ShapeDtypeStruct((cols, E), F32), sums)
        extra = ()
    else:
        out = (
            jax.ShapeDtypeStruct((n * R, E), BF16),
            jax.ShapeDtypeStruct((6 * R, E), F32),
            jax.ShapeDtypeStruct((2 * R, E), BF16),
            sums,
        )
        extra = (dv_in,)
    return vmem_call(
        functools.partial(pair_kernel, chunks, first), out,
        scratch=(
            pltpu.VMEM((cols, E), BF16),
            pltpu.VMEM((n * R, E), BF16),
            pltpu.VMEM((n * R, cols), BF16),
            pltpu.VMEM((2, max(chunks) * R, cols), F32),
        ),
        smem_first=True, n_in=1 + n + 6 + len(extra),
        flops=6 * n * R * cols * E, nbytes=4 * (n * R + cols) * E,
    )(scal, *us, *vs, *extra)


def back_kernel(
    scal_ref, ui_ref, ni_ref, du_ref, qa_ref, qb_ref, ut_ref, nt_ref, dv_ref, px_ref,
    di_ref, dt_ref, keep_ref, send_ref,
):
    scale = scal_ref[0, 0]
    low = scal_ref[0, 1] == 0.0
    du = scale * (du_ref[...] + qa_ref[...].astype(F32) + qb_ref[...].astype(F32))
    dv = scale * (dv_ref[...] + px_ref[...].astype(F32))
    for k, (unit_ref, norm_ref, grad, out_ref) in enumerate(
        ((ui_ref, ni_ref, du, di_ref), (ut_ref, nt_ref, dv, dt_ref))
    ):
        unit = unit_ref[...]
        d = (grad - unit * jnp.sum(unit * grad, axis=1, keepdims=True)) / norm_ref[...]
        out_ref[...] = d.astype(BF16)
        left, right = d[:, :H], d[:, H:]
        keep_ref[k * R : (k + 1) * R] = jnp.where(low, left, right).astype(BF16)
        send_ref[k * R : (k + 1) * R] = jnp.where(low, right, left).astype(BF16)


def back(scal, *args):
    low = jax.ShapeDtypeStruct((R, E), BF16)
    half = jax.ShapeDtypeStruct((2 * R, H), BF16)
    return vmem_call(
        back_kernel, (low, low, half, half), smem_first=True, n_in=10,
        flops=20 * R * E, nbytes=30 * R * E,
    )(scal, *args)


def input_grad_kernel(di_ref, dt_ref, head_ref, gi_ref, gt_ref):
    head = head_ref[...]
    gi_ref[...] = dot(di_ref[...], head, NT).astype(BF16)
    gt_ref[...] = dot(dt_ref[...], head, NT).astype(BF16)


def input_grad(di, dt, head):
    out = jax.ShapeDtypeStruct((R, D), BF16)
    return vmem_call(
        input_grad_kernel, (out, out), n_in=3, flops=4 * R * D * E, nbytes=2 * (4 * R * D + D * E)
    )(di, dt, head)


ZROWS = 24
PAD = 16


def head_grad_kernel(x_ref, y_ref, ox_ref, oy_ref, keep_ref, got_ref, extra_ref, out_ref, x_all, d_all):
    for i, ref in enumerate((x_ref, y_ref, ox_ref, oy_ref)):
        x_all[i * R : (i + 1) * R] = ref[...]
    d_all[: 2 * R] = keep_ref[...]
    d_all[2 * R :] = got_ref[...]
    d = d_all[...]
    for xl in range(2):
        full = dot(x_all[:, xl * E : (xl + 1) * E], d, TN)
        for y in range(4):
            for z in range(0, 8, 2):
                a = (z * 4 + y) * ZROWS
                b = ((z + 1) * 4 + y) * ZROWS
                both = jnp.concatenate([full[a : a + ZROWS], full[b : b + ZROWS]], axis=0)
                out_ref[xl * 4 + y, z * ZROWS : (z + 2) * ZROWS] = both.astype(BF16)
    for j in range(8):
        out_ref[j, 8 * ZROWS :] = extra_ref[...]


def head_grad_parts(x, y, ox, oy, keep, got, extra):
    return vmem_call(
        head_grad_kernel, jax.ShapeDtypeStruct((8, 8 * ZROWS + PAD, H), BF16),
        scratch=(pltpu.VMEM((4 * R, D), BF16), pltpu.VMEM((4 * R, H), BF16)),
        n_in=7, flops=8 * R * D * H, nbytes=2 * (4 * R * D + D * H),
    )(x, y, ox, oy, keep, got, extra)


def swap(axis):
    return lambda v: lax.ppermute(v, axis, [(0, 1), (1, 0)])


def ring(axis, n):
    even = [(i, i ^ 1) for i in range(n)]
    odd = [(i, (i + 1) % n if i % 2 else (i - 1) % n) for i in range(n)]
    return (lambda v: lax.ppermute(v, axis, even)), (lambda v: lax.ppermute(v, axis, odd))


def split3(t):
    hi = lax.reduce_precision(t, 8, 7)
    mid = lax.reduce_precision(t - hi, 8, 7)
    return hi, mid, t - hi - mid


def scalar_rows(t, rows):
    parts = jnp.stack(split3(t))
    return jnp.concatenate([parts, jnp.zeros((rows - 3, H), F32)]).astype(BF16)


def per_device(image, text, log_scale, bias, head):
    x = image[0]
    y = text[0]
    scale = jnp.exp(log_scale)
    core = lax.axis_index("c")
    z1, z2 = ring("z", 8)
    y1, y2 = ring("y", 4)
    xl = swap("xl")
    cc = swap("c")

    ui, ni, u, ut, nt, v = project(x, y, head)

    vx = xl(v)
    a1, b1 = z1(u), z2(u)
    w = jnp.concatenate([v, vx])
    wa, wb = y1(w), y2(w)
    a2, b2 = z1(b1), z2(a1)
    wfa, wfb = y1(wb[:R]), y2(wa[R:])
    a3, b3 = z1(b2), z2(a2)
    fa, fb = z1(b3[: R // 2]), z2(a3[R // 2 :])
    vs = (v, vx, wa, wb, wfa, wfb)
    ox, oy = cc(x), cc(y)

    scal = jnp.stack([scale * LOG2E, bias * LOG2E]).reshape(1, 2)
    du, dv, sums1 = pair((1, 2, 2, 2), True, scal, (u, a1, b1, a2, b2, a3, b3), vs)
    far = jnp.concatenate([fa, fb])
    duf, dvn, dvf, sums2 = pair((1,), False, scal, (far,), vs, dv)

    ra, rb = z1(duf[: R // 2]), z2(duf[R // 2 :])
    sa, sb = y1(dvf[:R]), y2(dvf[R:])
    p = [du[i * R : (i + 1) * R] for i in range(7)]
    pad = jnp.zeros((R // 2, E), BF16)
    ra = jnp.concatenate([ra, pad]).astype(F32)
    rb = jnp.concatenate([pad, rb]).astype(F32)
    qa, qb = z1((p[5] + rb).astype(BF16)), z2((p[6] + ra).astype(BF16))
    pad = jnp.zeros((R, E), BF16)
    sa = jnp.concatenate([sa, pad]).astype(F32)
    sb = jnp.concatenate([pad, sb]).astype(F32)
    ta, tb = y1((dvn[2 * R : 4 * R] + sb).astype(BF16)), y2((dvn[4 * R : 6 * R] + sa).astype(BF16))
    qa, qb = z1((p[3] + qb).astype(BF16)), z2((p[4] + qa).astype(BF16))
    wsum = dvn[: 2 * R] + ta.astype(F32) + tb.astype(F32)
    px = xl(wsum[R:].astype(BF16))
    qa, qb = z1((p[1] + qb).astype(BF16)), z2((p[2] + qa).astype(BF16))

    sums = jnp.sum(sums1 + sums2, axis=(1, 2))
    extra = scalar_rows(jnp.zeros((H,), F32).at[:3].set(sums), PAD)

    scal2 = jnp.stack([scale, core.astype(F32)]).reshape(1, 2)
    di, dt, keep, send = back(scal2, ui, ni, p[0], qa, qb, ut, nt, wsum[:R], px)
    got = cc(send)
    gi, gt = input_grad(di, dt, head)

    parts = head_grad_parts(x, y, ox, oy, keep, got, extra)
    parts = lax.all_to_all(parts, ("xl", "y"), 0, 0, tiled=True)
    s = jnp.sum(parts.astype(F32), axis=0)
    t = jnp.sum(s[8 * ZROWS : 8 * ZROWS + 3], axis=0)
    rows = jnp.broadcast_to(scalar_rows(t, 8)[None], (8, 8, H))
    parts = jnp.concatenate([s[: 8 * ZROWS].reshape(8, ZROWS, H).astype(BF16), rows], axis=1)
    parts = lax.all_to_all(parts, "z", 0, 0, tiled=True)
    s = jnp.sum(parts.astype(F32), axis=0)
    s = s + swap("xh")(s)
    o = cc(s)
    hg = jnp.where(
        core == 0,
        jnp.concatenate([s[:ZROWS], o[:ZROWS]], axis=1),
        jnp.concatenate([o[:ZROWS], s[:ZROWS]], axis=1),
    )
    t = jnp.sum(s[ZROWS : ZROWS + 3, :3] + o[ZROWS : ZROWS + 3, :3], axis=0)
    count = float(4 * 8192) * 8192.0
    return t[0] / count, scale * t[1] / count, t[2] / count, gi[None], gt[None], hg


def solution(mesh):
    fine = Mesh(mesh.devices.reshape(2, 8, 4, 2, 2), ("xl", "z", "y", "xh", "c"))
    blk = ("xl", "z", "y")
    rep = ("xh", "c")
    data = P(rep, blk, None)
    return jax.shard_map(
        per_device,
        mesh=fine,
        in_specs=(data, data, P(), P(), P()),
        out_specs=(P(), P(), P(), data, data, P(blk, None)),
        check_vma=False,
    )
```

```python
import functools
import math

import jax
import jax.numpy as jnp
from jax import lax
from jax.experimental import pallas as pl
from jax.experimental.pallas import tpu as pltpu
from jax.sharding import Mesh, PartitionSpec as P

F32 = jnp.float32
BF16 = jnp.bfloat16
LOG2E = 1.4426950408889634
LN2 = 0.6931471805599453
R = 128
E = 768
D = 1536
H = E // 2

NT = (((1,), (1,)), ((), ()))
NN = (((1,), (0,)), ((), ()))
TN = (((0,), (0,)), ((), ()))


def dot(a, b, dims):
    return lax.dot_general(a, b, dims, preferred_element_type=F32)


GRANT = 6 << 20
VM = pl.BlockSpec(memory_space=pltpu.VMEM)
SM = pl.BlockSpec(memory_space=pltpu.SMEM)
HB = pl.BlockSpec(memory_space=pltpu.HBM)
VP = pl.BlockSpec(memory_space=pltpu.VMEM, index_map=None)


def vmem_call(kernel, out_shape, scratch=(), smem=0, n_in=0, flops=0, nbytes=0, specs=None, out_specs=None):
    if specs is None:
        specs = [SM] * smem + [VM] * (n_in - smem)
    if out_specs is None:
        out_specs = jax.tree.map(lambda _: VM, out_shape)

    def place_out(t, spec):
        if spec is HB:
            return pltpu.HBM(t.shape, t.dtype)
        if spec is VP:
            return pltpu.VMEM(t.shape, t.dtype)
        return t

    def place_in(t, spec):
        if spec is HB:
            return pltpu.with_memory_space_constraint(t, pltpu.HBM)
        if spec is VP:
            return pltpu.with_memory_space_constraint(t, pltpu.VMEM)
        return t

    def call(*args):
        held = sum(t.size * jnp.dtype(t.dtype).itemsize for t in (*args, *jax.tree.leaves(out_shape)))
        held += sum(4 * math.prod(t.shape) for t in scratch)
        return pl.pallas_call(
            kernel,
            out_shape=jax.tree.map(place_out, out_shape, out_specs),
            in_specs=specs,
            out_specs=out_specs,
            scratch_shapes=list(scratch),
            compiler_params=pltpu.CompilerParams(vmem_limit_bytes=2 * held + GRANT),
            cost_estimate=pl.CostEstimate(flops=flops, bytes_accessed=nbytes, transcendentals=0),
        )(*(place_in(t, spec) for t, spec in zip(args, specs)))

    return call


PARTS = 3


def proj_kernel(copies, x_hbm, head_hbm, *refs):
    b_ref, unit_hbm, norm_hbm, x_v, head_v, unit_v, norm_v, low_v, in_sem, out_sem = refs[-10:]
    deep = D // PARTS
    get_x = pltpu.make_async_copy(x_hbm, x_v, in_sem.at[PARTS])
    get = [
        pltpu.make_async_copy(head_hbm.at[pl.ds(k * deep, deep)], head_v.at[pl.ds(k * deep, deep)], in_sem.at[k])
        for k in range(PARTS)
    ]
    get_x.start()
    for c in get:
        c.start()
    get_x.wait()
    proj = None
    for k, c in enumerate(get):
        c.wait()
        part = dot(x_v[:, k * deep : (k + 1) * deep], head_v[k * deep : (k + 1) * deep], NN)
        proj = part if proj is None else proj + part
    norm = jnp.sqrt(jnp.sum(proj * proj, axis=1, keepdims=True) + 1e-06)
    unit = proj / norm
    unit_v[...] = unit
    norm_v[...] = jnp.broadcast_to(norm, (R, 128))
    put = [
        pltpu.make_async_copy(unit_v, unit_hbm, out_sem.at[0]),
        pltpu.make_async_copy(norm_v, norm_hbm, out_sem.at[1]),
    ]
    for c in put:
        c.start()
    low = unit.astype(BF16)
    if copies == 1:
        b_ref[...] = low
    else:
        low_v[...] = low
        for k in range(copies):
            put.append(pltpu.make_async_copy(low_v, b_ref.at[pl.ds(k * R, R)], out_sem.at[2 + k]))
            put[-1].start()
    for c in put:
        c.wait()


def project(copies, x, head, after=()):
    return vmem_call(
        functools.partial(proj_kernel, copies),
        (
            jax.ShapeDtypeStruct((copies * R, E), BF16),
            jax.ShapeDtypeStruct((R, E), F32),
            jax.ShapeDtypeStruct((R, 128), F32),
        ),
        scratch=(
            pltpu.VMEM((R, D), BF16),
            pltpu.VMEM((D, E), BF16),
            pltpu.VMEM((R, E), F32),
            pltpu.VMEM((R, 128), F32),
            pltpu.VMEM((R, E), BF16),
            pltpu.SemaphoreType.DMA((PARTS + 1,)),
            pltpu.SemaphoreType.DMA((2 + copies,)),
        ),
        specs=[HB] * (2 + len(after)), out_specs=(HB if copies > 1 else VM, HB, HB),
        flops=2 * R * D * E, nbytes=2 * (R * D + D * E),
    )(x, head, *after)


SUB = 8
CB = 256
RB = 32


def pair_elementwise(s_ref, g_ref, rows, scale2, bias2, diag_at):
    acc_m = jnp.zeros((SUB, CB), F32)
    acc_l = jnp.zeros((SUB, CB), F32)
    acc_s = jnp.zeros((SUB, CB), F32)
    acc_g = jnp.zeros((SUB, CB), F32)

    def fold(t):
        return jnp.sum(t.reshape(RB // SUB, SUB, CB), axis=0)

    for c in range(s_ref.shape[1] // CB):
        prod = jnp.ones((SUB, CB), F32)
        for r in range(rows // RB):
            s = s_ref[r * RB : (r + 1) * RB, c * CB : (c + 1) * CB]
            z = s * scale2 + bias2
            if diag_at is not None:
                row = r * RB + lax.broadcasted_iota(jnp.int32, (RB, CB), 0)
                col = c * CB + lax.broadcasted_iota(jnp.int32, (RB, CB), 1)
                mask = row + diag_at == col
                z = jnp.where(mask, -z, z)
            t = jnp.exp2(-jnp.abs(z))
            one_t = 1.0 + t
            inv = 1.0 / one_t
            g = jnp.where(z >= 0.0, inv, t * inv)
            if diag_at is not None:
                g = jnp.where(mask, -g, g)
            g_ref[r * RB : (r + 1) * RB, c * CB : (c + 1) * CB] = g.astype(BF16)
            acc_m = acc_m + fold(jnp.maximum(z, 0.0))
            acc_s = acc_s + fold(g * s)
            acc_g = acc_g + fold(g)
            for k in range(RB // SUB):
                prod = prod * one_t[k * SUB : (k + 1) * SUB]
        acc_l = acc_l + jnp.log(prod)
    return LN2 * acc_m + acc_l, acc_s, acc_g


def pair_kernel(chunks, own, scal_ref, at_ref, v_ref, *refs):
    n = sum(len(c) for c in chunks)
    if not own:
        before_ref, refs = refs[0], refs[1:]
    u_refs, du_refs, (g_ref, sums_ref, u_all, s_all) = refs[:n], refs[n : 2 * n], refs[2 * n :]
    scale2 = scal_ref[0, 0]
    bias2 = scal_ref[0, 1]
    v = v_ref[...]
    tot = None
    at = 0
    for i, chunk in enumerate(chunks):
        rows = 0
        for k in chunk:
            u_all[i % 2, rows : rows + u_refs[k].shape[0]] = u_refs[k][...]
            rows += u_refs[k].shape[0]
        s_all[i % 2, :rows] = dot(u_all[i % 2, :rows], v, NT)
        part = pair_elementwise(
            s_all.at[i % 2], g_ref.at[pl.ds(at, rows)], rows, scale2, bias2,
            at_ref[0, 0] if own and i == 0 else None,
        )
        tot = part if tot is None else tuple(a + b for a, b in zip(tot, part))
        du = dot(g_ref[at : at + rows], v, NN)
        at += rows
        rows = 0
        for k in chunk:
            ref = du_refs[k]
            ref[...] = du[rows : rows + ref.shape[0]].astype(ref.dtype)
            rows += ref.shape[0]
    for i in range(3):
        sums_ref[i] = tot[i] if own else tot[i] + before_ref[i]


def pair(chunks, own, scal, at, v, us, dtype, before=()):
    rows = sum(u.shape[0] for u in us)
    most = max(sum(us[k].shape[0] for k in c) for c in chunks)
    cols = v.shape[0]
    out = (
        *(jax.ShapeDtypeStruct(u.shape, dtype) for u in us),
        jax.ShapeDtypeStruct((rows, cols), BF16),
        jax.ShapeDtypeStruct((3, SUB, CB), F32),
    )
    return vmem_call(
        functools.partial(pair_kernel, chunks, own), out,
        scratch=(pltpu.VMEM((2, most, E), BF16), pltpu.VMEM((2, most, cols), F32)),
        specs=[SM, SM] + [VM] * (1 + len(before) + len(us)), out_specs=(VP,) * (len(us) + 2),
        flops=4 * rows * cols * E, nbytes=4 * (rows + cols) * E,
    )(scal, at, v, *before, *us)


def cols_kernel(*refs):
    n = len(refs) - 6
    g1_ref, g2_ref, u_refs, (dv_hbm, u_all, dv_ref, sem) = refs[0], refs[1], refs[2 : 2 + n], refs[-4:]
    at = 0
    for ref in u_refs:
        u_all[at : at + ref.shape[0]] = ref[...]
        at += ref.shape[0]
    k = g1_ref.shape[0]
    cols = dv_ref.shape[0] // 2
    put = []
    for i in range(2):
        at = pl.ds(i * cols, cols)
        dv = dot(g1_ref[:, at], u_all[:k], TN) + dot(g2_ref[:, at], u_all[k:], TN)
        dv_ref[at] = dv.astype(BF16)
        put.append(pltpu.make_async_copy(dv_ref.at[at], dv_hbm.at[at], sem.at[i]))
        put[i].start()
    for c in put:
        c.wait()


def pair_cols(g1, g2, us):
    rows = g1.shape[0] + g2.shape[0]
    cols = g1.shape[1]
    return vmem_call(
        cols_kernel, jax.ShapeDtypeStruct((cols, E), BF16),
        scratch=(pltpu.VMEM((rows, E), BF16), pltpu.VMEM((cols, E), BF16), pltpu.SemaphoreType.DMA((2,))),
        specs=[VP, VP] + [VM] * len(us), out_specs=HB,
        flops=2 * rows * cols * E, nbytes=2 * (rows * cols + rows * E + cols * E),
    )(g1, g2, *us)


def step_kernel(pa_ref, pb_ref, ra_ref, rb_ref, a_ref, b_ref):
    half = ra_ref.shape[0]
    if half == R:
        a_ref[...] = (pa_ref[...] + rb_ref[...].astype(F32)).astype(BF16)
        b_ref[...] = (pb_ref[...] + ra_ref[...].astype(F32)).astype(BF16)
    else:
        a_ref[:half] = pa_ref[:half].astype(BF16)
        a_ref[half:] = (pa_ref[half:] + rb_ref[...].astype(F32)).astype(BF16)
        b_ref[:half] = (pb_ref[:half] + ra_ref[...].astype(F32)).astype(BF16)
        b_ref[half:] = pb_ref[half:].astype(BF16)


STEP_FLOPS = 8 * 10**9


def ring_step(pa, pb, ra, rb):
    low = jax.ShapeDtypeStruct((R, E), BF16)
    return vmem_call(step_kernel, (low, low), specs=[VP, VP, VM, VM], flops=STEP_FLOPS, nbytes=16 * R * E)(pa, pb, ra, rb)


def back_kernel(
    scal_ref, ui_hbm, ni_hbm, ut_hbm, nt_hbm, du_ref, qa_ref, qb_ref, dv_ref,
    di_ref, dt_ref, keep_ref, send_ref, ui_ref, ni_ref, ut_ref, nt_ref, sem,
):
    get = [
        pltpu.make_async_copy(src, dst, sem.at[k])
        for k, (src, dst) in enumerate(
            ((ui_hbm, ui_ref), (ni_hbm, ni_ref), (ut_hbm, ut_ref), (nt_hbm, nt_ref))
        )
    ]
    for c in get:
        c.start()
    scale = scal_ref[0, 0]
    low = scal_ref[0, 1] == 0.0
    du = scale * (du_ref[...] + qa_ref[...].astype(F32) + qb_ref[...].astype(F32))
    dv = dv_ref[:R].astype(F32)
    for j in range(1, 8):
        dv = dv + dv_ref[j * R : (j + 1) * R].astype(F32)
    dv = scale * dv
    for c in get:
        c.wait()
    for k, (unit_ref, norm_ref, grad, out_ref) in enumerate(
        ((ui_ref, ni_ref, du, di_ref), (ut_ref, nt_ref, dv, dt_ref))
    ):
        unit = unit_ref[...]
        d = (grad - unit * jnp.sum(unit * grad, axis=1, keepdims=True)) / norm_ref[:, :1]
        out_ref[...] = d.astype(BF16)
        left, right = d[:, :H], d[:, H:]
        keep_ref[k * R : (k + 1) * R] = jnp.where(low, left, right).astype(BF16)
        send_ref[k * R : (k + 1) * R] = jnp.where(low, right, left).astype(BF16)


def back(scal, *args):
    low = jax.ShapeDtypeStruct((R, E), BF16)
    half = jax.ShapeDtypeStruct((2 * R, H), BF16)
    return vmem_call(
        back_kernel, (low, low, half, half), specs=[SM] + [HB] * 4 + [VP] + [VM] * 3,
        scratch=(
            pltpu.VMEM((R, E), F32),
            pltpu.VMEM((R, 128), F32),
            pltpu.VMEM((R, E), F32),
            pltpu.VMEM((R, 128), F32),
            pltpu.SemaphoreType.DMA((4,)),
        ),
        flops=20 * R * E, nbytes=30 * R * E,
    )(scal, *args)


def input_grad_kernel(di_ref, dt_ref, head_ref, gi_ref, gt_ref, done_ref):
    head = head_ref[...]
    done_ref[...] = jnp.zeros((8, 128), F32)
    gi_ref[...] = dot(di_ref[...], head, NT).astype(BF16)
    gt_ref[...] = dot(dt_ref[...], head, NT).astype(BF16)


def input_grad(di, dt, head):
    out = jax.ShapeDtypeStruct((R, D), BF16)
    return vmem_call(
        input_grad_kernel, (out, out, jax.ShapeDtypeStruct((8, 128), F32)), n_in=3, flops=4 * R * D * E, nbytes=2 * (4 * R * D + D * E)
    )(di, dt, head)


ZROWS = 24
PAD = 16


def head_grad_kernel(x_hbm, y_hbm, ox_hbm, oy_hbm, keep_ref, got_ref, extra_ref, out_hbm, x_all, d_all, out_v, in_sem, out_sem):
    get = []
    for i, src in enumerate((x_hbm, y_hbm, ox_hbm, oy_hbm)):
        get.append(pltpu.make_async_copy(src, x_all.at[pl.ds(i * R, R)], in_sem.at[i]))
        get[i].start()
    d_all[: 2 * R] = keep_ref[...]
    d_all[2 * R :] = got_ref[...]
    for j in range(8):
        out_v[j, 8 * ZROWS :] = extra_ref[...]
    d = d_all[...]
    for c in get:
        c.wait()
    put = []
    for xl in range(2):
        full = dot(x_all[:, xl * E : (xl + 1) * E], d, TN)
        for y in range(4):
            for z in range(0, 8, 2):
                a = (z * 4 + y) * ZROWS
                b = ((z + 1) * 4 + y) * ZROWS
                both = jnp.concatenate([full[a : a + ZROWS], full[b : b + ZROWS]], axis=0)
                out_v[xl * 4 + y, z * ZROWS : (z + 2) * ZROWS] = both.astype(BF16)
        at = pl.ds(xl * 4, 4)
        put.append(pltpu.make_async_copy(out_v.at[at], out_hbm.at[at], out_sem.at[xl]))
        put[xl].start()
    for c in put:
        c.wait()


def head_grad_parts(x, y, ox, oy, keep, got, extra):
    shape = (8, 8 * ZROWS + PAD, H)
    return vmem_call(
        head_grad_kernel, jax.ShapeDtypeStruct(shape, BF16),
        scratch=(
            pltpu.VMEM((4 * R, D), BF16),
            pltpu.VMEM((4 * R, H), BF16),
            pltpu.VMEM(shape, BF16),
            pltpu.SemaphoreType.DMA((4,)),
            pltpu.SemaphoreType.DMA((2,)),
        ),
        specs=[HB] * 4 + [VM] * 3, out_specs=HB, flops=8 * R * D * H, nbytes=2 * (4 * R * D + D * H),
    )(x, y, ox, oy, keep, got, extra)


def sum_kernel(parts_ref, _, out_ref):
    s = parts_ref[0].astype(F32)
    for j in range(1, 8):
        s = s + parts_ref[j].astype(F32)
    t = jnp.sum(s[8 * ZROWS : 8 * ZROWS + 3], axis=0, keepdims=True)
    hi = t.astype(BF16).astype(F32)
    mid = (t - hi).astype(BF16).astype(F32)
    low = t - hi - mid
    row = lax.broadcasted_iota(jnp.int32, (8, H), 0)
    tail = jnp.where(row == 0, hi, jnp.where(row == 1, mid, jnp.where(row == 2, low, 0.0)))
    for z in range(8):
        out_ref[z] = jnp.concatenate([s[z * ZROWS : (z + 1) * ZROWS], tail], axis=0).astype(BF16)


def sum_parts(parts, after):
    return vmem_call(
        sum_kernel, jax.ShapeDtypeStruct((8, ZROWS + 8, H), BF16), n_in=2,
        flops=10 * parts.size, nbytes=2 * parts.size,
    )(parts, after)


def last_kernel(scal_ref, s_ref, r_ref, o_ref, hg_ref, l_ref, a_ref, b_ref):
    low = scal_ref[0, 1] == 0.0
    mine = s_ref[...] + r_ref[...]
    other = o_ref[...]
    left = jnp.where(low, mine, other)
    right = jnp.where(low, other, mine)
    hg_ref[:, :H] = left[:ZROWS]
    hg_ref[:, H:] = right[:ZROWS]
    t = jnp.sum((mine + other)[ZROWS : ZROWS + 3], axis=0, keepdims=True) * (1.0 / COUNT)
    l_ref[...] = t[:, 0:1]
    a_ref[...] = scal_ref[0, 0] * t[:, 1:2]
    b_ref[...] = t[:, 2:3]


COUNT = float(4 * 8192) * 8192.0


def last(scal, s, r, o):
    one = jax.ShapeDtypeStruct((1, 1), F32)
    return vmem_call(
        last_kernel, (jax.ShapeDtypeStruct((ZROWS, E), F32), one, one, one), smem=1, n_in=4,
        flops=ZROWS * E, nbytes=16 * ZROWS * E,
    )(scal, s, r, o)


def swap(axis):
    return lambda v: lax.ppermute(v, axis, [(0, 1), (1, 0)])


def ring(axis, n):
    even = [(i, i ^ 1) for i in range(n)]
    odd = [(i, (i + 1) % n if i % 2 else (i - 1) % n) for i in range(n)]
    return (lambda v: lax.ppermute(v, axis, even)), (lambda v: lax.ppermute(v, axis, odd))


def split3(t):
    hi = lax.reduce_precision(t, 8, 7)
    mid = lax.reduce_precision(t - hi, 8, 7)
    return hi, mid, t - hi - mid


def scalar_rows(t, rows):
    parts = jnp.stack(split3(t))
    return jnp.concatenate([parts, jnp.zeros((rows - 3, H), F32)]).astype(BF16)


def per_device(image, text, log_scale, bias, head):
    x = image[0]
    y = text[0]
    scale = jnp.exp(log_scale)
    core = lax.axis_index("c")
    z1, z2 = ring("z", 8)
    cc = swap("c")
    near = ("xl", "y")

    u, ui, ni = project(1, x, head)
    a1, b1 = z1(u), z2(u)
    v, ut, nt = project(8, y, head, (ni,))

    vs = lax.all_to_all(v, near, 0, 0, tiled=True)
    a2, b2 = z1(b1), z2(a1)
    a3, b3 = z1(b2), z2(a2)
    fa, fb = z1(b3[: R // 2]), z2(a3[R // 2 :])
    ox, oy = cc(x), cc(y)

    scal = jnp.stack([scale * LOG2E, bias * LOG2E]).reshape(1, 2)
    at = (lax.axis_index(near) * R).reshape(1, 1)
    us = (u, a1, b1, a2, b2, a3, b3)
    *p, g1, sums = pair(((0,), (1, 2), (3, 4), (5, 6)), True, scal, at, vs, us, F32)
    qa, qb, g2, sums = pair(((0, 1),), False, scal, at, vs, (fa, fb), BF16, (sums,))

    qa, qb = z1(qa), z2(qb)
    dv = lax.all_to_all(pair_cols(g1, g2, (*us, fa, fb)), near, 0, 0, tiled=True)
    for k in (5, 3, 1):
        qa, qb = ring_step(p[k], p[k + 1], qa, qb)
        qa, qb = z1(qa), z2(qb)

    sums = jnp.sum(sums, axis=(1, 2))
    extra = scalar_rows(jnp.zeros((H,), F32).at[:3].set(sums), PAD)

    scal2 = jnp.stack([scale, core.astype(F32)]).reshape(1, 2)
    di, dt, keep, send = back(scal2, ui, ni, ut, nt, p[0], qa, qb, dv)
    got = cc(send)
    gi, gt, done = input_grad(di, dt, head)

    parts = head_grad_parts(x, y, ox, oy, keep, got, extra)
    parts = lax.all_to_all(parts, ("xl", "y"), 0, 0, tiled=True)
    parts = lax.all_to_all(sum_parts(parts, done), "z", 0, 0, tiled=True)
    s = jnp.sum(parts.astype(F32), axis=0)
    r = swap("xh")(s)
    o = cc(s + r)
    hg, l, a, b = last(scal2, s, r, o)
    return l.reshape(()), a.reshape(()), b.reshape(()), gi[None], gt[None], hg


def solution(mesh):
    fine = Mesh(mesh.devices.reshape(2, 8, 4, 2, 2), ("xl", "z", "y", "xh", "c"))
    blk = ("xl", "z", "y")
    rep = ("xh", "c")
    data = P(rep, blk, None)
    return jax.shard_map(
        per_device,
        mesh=fine,
        in_specs=(data, data, P(), P(), P()),
        out_specs=(P(), P(), P(), data, data, P(blk, None)),
        check_vma=False,
    )
```

```python
import functools
import math

import jax
import jax.numpy as jnp
from jax import lax
from jax.experimental import pallas as pl
from jax.experimental.pallas import tpu as pltpu
from jax.sharding import Mesh, PartitionSpec as P

F32 = jnp.float32
BF16 = jnp.bfloat16
LOG2E = 1.4426950408889634
LN2 = 0.6931471805599453
R = 128
E = 768
D = 1536
H = E // 2

NT = (((1,), (1,)), ((), ()))
NN = (((1,), (0,)), ((), ()))
TN = (((0,), (0,)), ((), ()))


def dot(a, b, dims):
    return lax.dot_general(a, b, dims, preferred_element_type=F32)


GRANT = 6 << 20
VM = pl.BlockSpec(memory_space=pltpu.VMEM)
SM = pl.BlockSpec(memory_space=pltpu.SMEM)
HB = pl.BlockSpec(memory_space=pltpu.HBM)
VP = pl.BlockSpec(memory_space=pltpu.VMEM, index_map=None)


def vmem_call(kernel, out_shape, scratch=(), smem=0, n_in=0, flops=0, nbytes=0, specs=None, out_specs=None):
    if specs is None:
        specs = [SM] * smem + [VM] * (n_in - smem)
    if out_specs is None:
        out_specs = jax.tree.map(lambda _: VM, out_shape)

    def place_out(t, spec):
        if spec is HB:
            return pltpu.HBM(t.shape, t.dtype)
        if spec is VP:
            return pltpu.VMEM(t.shape, t.dtype)
        return t

    def place_in(t, spec):
        if spec is HB:
            return pltpu.with_memory_space_constraint(t, pltpu.HBM)
        if spec is VP:
            return pltpu.with_memory_space_constraint(t, pltpu.VMEM)
        return t

    def call(*args):
        held = sum(t.size * jnp.dtype(t.dtype).itemsize for t in (*args, *jax.tree.leaves(out_shape)))
        held += sum(4 * math.prod(t.shape) for t in scratch)
        return pl.pallas_call(
            kernel,
            out_shape=jax.tree.map(place_out, out_shape, out_specs),
            in_specs=specs,
            out_specs=out_specs,
            scratch_shapes=list(scratch),
            compiler_params=pltpu.CompilerParams(vmem_limit_bytes=2 * held + GRANT),
            cost_estimate=pl.CostEstimate(flops=flops, bytes_accessed=nbytes, transcendentals=0),
        )(*(place_in(t, spec) for t, spec in zip(args, specs)))

    return call


PARTS = 3


def proj_kernel(
    x_hbm, y_hbm, head_hbm, u_ref, v_hbm, ui_hbm, ni_hbm, ut_hbm, nt_hbm,
    x_v, y_v, head_v, unit_v, norm_v, low_v, in_sem, out_sem,
):
    deep = D // PARTS
    get_x = pltpu.make_async_copy(x_hbm, x_v, in_sem.at[PARTS])
    get_y = pltpu.make_async_copy(y_hbm, y_v, in_sem.at[PARTS + 1])
    get = [
        pltpu.make_async_copy(head_hbm.at[pl.ds(k * deep, deep)], head_v.at[pl.ds(k * deep, deep)], in_sem.at[k])
        for k in range(PARTS)
    ]
    get_y.start()
    for c in get:
        c.start()
    get_x.start()
    put = []

    def send(src, dst):
        put.append(pltpu.make_async_copy(src, dst, out_sem.at[len(put)]))
        put[-1].start()

    def finish(k, proj, unit_hbm, norm_hbm):
        norm = jnp.sqrt(jnp.sum(proj * proj, axis=1, keepdims=True) + 1e-06)
        unit = proj / norm
        unit_v[k] = unit
        norm_v[k] = jnp.broadcast_to(norm, (R, 128))
        send(unit_v.at[k], unit_hbm)
        send(norm_v.at[k], norm_hbm)
        return unit.astype(BF16)

    get_y.wait()
    proj = None
    for k, c in enumerate(get):
        c.wait()
        part = dot(y_v[:, k * deep : (k + 1) * deep], head_v[k * deep : (k + 1) * deep], NN)
        proj = part if proj is None else proj + part
    low_v[...] = finish(0, proj, ut_hbm, nt_hbm)
    for k in range(8):
        send(low_v, v_hbm.at[pl.ds(k * R, R)])
    get_x.wait()
    u_ref[...] = finish(1, dot(x_v[...], head_v[...], NN), ui_hbm, ni_hbm)
    for c in put:
        c.wait()


def project(x, y, head):
    unit = jax.ShapeDtypeStruct((R, E), F32)
    norm = jax.ShapeDtypeStruct((R, 128), F32)
    return vmem_call(
        proj_kernel,
        (jax.ShapeDtypeStruct((R, E), BF16), jax.ShapeDtypeStruct((8 * R, E), BF16), unit, norm, unit, norm),
        scratch=(
            pltpu.VMEM((R, D), BF16),
            pltpu.VMEM((R, D), BF16),
            pltpu.VMEM((D, E), BF16),
            pltpu.VMEM((2, R, E), F32),
            pltpu.VMEM((2, R, 128), F32),
            pltpu.VMEM((R, E), BF16),
            pltpu.SemaphoreType.DMA((PARTS + 2,)),
            pltpu.SemaphoreType.DMA((12,)),
        ),
        specs=[HB] * 3, out_specs=(VM, HB, HB, HB, HB, HB),
        flops=4 * R * D * E, nbytes=2 * (2 * R * D + D * E),
    )(x, y, head)


SUB = 8
CB = 256
RB = 32


def pair_elementwise(s_ref, g_ref, rows, scale2, bias2, diag_at):
    acc_m = jnp.zeros((SUB, CB), F32)
    acc_l = jnp.zeros((SUB, CB), F32)
    acc_s = jnp.zeros((SUB, CB), F32)
    acc_g = jnp.zeros((SUB, CB), F32)

    def fold(t):
        return jnp.sum(t.reshape(RB // SUB, SUB, CB), axis=0)

    for c in range(s_ref.shape[1] // CB):
        prod = jnp.ones((SUB, CB), F32)
        for r in range(rows // RB):
            s = s_ref[r * RB : (r + 1) * RB, c * CB : (c + 1) * CB]
            z = s * scale2 + bias2
            if diag_at is not None:
                row = r * RB + lax.broadcasted_iota(jnp.int32, (RB, CB), 0)
                col = c * CB + lax.broadcasted_iota(jnp.int32, (RB, CB), 1)
                mask = row + diag_at == col
                z = jnp.where(mask, -z, z)
            t = jnp.exp2(-jnp.abs(z))
            one_t = 1.0 + t
            inv = 1.0 / one_t
            g = jnp.where(z >= 0.0, inv, t * inv)
            if diag_at is not None:
                g = jnp.where(mask, -g, g)
            g_ref[r * RB : (r + 1) * RB, c * CB : (c + 1) * CB] = g.astype(BF16)
            acc_m = acc_m + fold(jnp.maximum(z, 0.0))
            acc_s = acc_s + fold(g * s)
            acc_g = acc_g + fold(g)
            for k in range(RB // SUB):
                prod = prod * one_t[k * SUB : (k + 1) * SUB]
        acc_l = acc_l + jnp.log(prod)
    return LN2 * acc_m + acc_l, acc_s, acc_g


def pair_kernel(chunks, own, scal_ref, at_ref, v_ref, *refs):
    n = sum(len(c) for c in chunks)
    if not own:
        before_ref, refs = refs[0], refs[1:]
    u_refs, du_refs, (g_ref, sums_ref, u_all, s_all) = refs[:n], refs[n : 2 * n], refs[2 * n :]
    scale2 = scal_ref[0, 0]
    bias2 = scal_ref[0, 1]
    v = v_ref[...]
    tot = None
    at = 0
    for i, chunk in enumerate(chunks):
        rows = 0
        for k in chunk:
            u_all[i % 2, rows : rows + u_refs[k].shape[0]] = u_refs[k][...]
            rows += u_refs[k].shape[0]
        s_all[i % 2, :rows] = dot(u_all[i % 2, :rows], v, NT)
        part = pair_elementwise(
            s_all.at[i % 2], g_ref.at[pl.ds(at, rows)], rows, scale2, bias2,
            at_ref[0, 0] if own and i == 0 else None,
        )
        tot = part if tot is None else tuple(a + b for a, b in zip(tot, part))
        du = dot(g_ref[at : at + rows], v, NN)
        at += rows
        rows = 0
        for k in chunk:
            ref = du_refs[k]
            ref[...] = du[rows : rows + ref.shape[0]].astype(ref.dtype)
            rows += ref.shape[0]
    for i in range(3):
        sums_ref[i] = tot[i] if own else tot[i] + before_ref[i]


def pair(chunks, own, scal, at, v, us, before=()):
    rows = sum(u.shape[0] for u in us)
    most = max(sum(us[k].shape[0] for k in c) for c in chunks)
    cols = v.shape[0]
    out = (
        *(jax.ShapeDtypeStruct(u.shape, BF16) for u in us),
        jax.ShapeDtypeStruct((rows, cols), BF16),
        jax.ShapeDtypeStruct((3, SUB, CB), F32),
    )
    return vmem_call(
        functools.partial(pair_kernel, chunks, own), out,
        scratch=(pltpu.VMEM((2, most, E), BF16), pltpu.VMEM((2, most, cols), F32)),
        specs=[SM, SM] + [VM] * (1 + len(before) + len(us)), out_specs=(VP,) * (len(us) + 2),
        flops=4 * rows * cols * E, nbytes=4 * (rows + cols) * E,
    )(scal, at, v, *before, *us)


def cols_kernel(*refs):
    n = len(refs) - 7
    g1_ref, g2_ref, u_refs, (dv_hbm, done_ref, u_all, dv_ref, sem) = refs[0], refs[1], refs[2 : 2 + n], refs[-5:]
    done_ref[...] = jnp.zeros(done_ref.shape, F32)
    at = 0
    for ref in u_refs:
        u_all[at : at + ref.shape[0]] = ref[...]
        at += ref.shape[0]
    k = g1_ref.shape[0]
    cols = dv_ref.shape[0] // 2
    put = []
    for i in range(2):
        at = pl.ds(i * cols, cols)
        dv = dot(g1_ref[:, at], u_all[:k], TN) + dot(g2_ref[:, at], u_all[k:], TN)
        dv_ref[at] = dv.astype(BF16)
        put.append(pltpu.make_async_copy(dv_ref.at[at], dv_hbm.at[at], sem.at[i]))
        put[i].start()
    for c in put:
        c.wait()


def pair_cols(g1, g2, us):
    rows = g1.shape[0] + g2.shape[0]
    cols = g1.shape[1]
    return vmem_call(
        cols_kernel, (jax.ShapeDtypeStruct((cols, E), BF16), jax.ShapeDtypeStruct((8, 128), F32)),
        scratch=(pltpu.VMEM((rows, E), BF16), pltpu.VMEM((cols, E), BF16), pltpu.SemaphoreType.DMA((2,))),
        specs=[VP, VP] + [VM] * len(us), out_specs=(HB, VM),
        flops=2 * rows * cols * E, nbytes=2 * (rows * cols + rows * E + cols * E),
    )(g1, g2, *us)


def step_kernel(n, *refs):
    for k in range(n):
        refs[-n + k][...] = (refs[k][...].astype(F32) + refs[n + k][...].astype(F32)).astype(BF16)


STEP_FLOPS = 8 * 10**9


def ring_step(own, got, after=()):
    n = len(own)
    return vmem_call(
        functools.partial(step_kernel, n), (jax.ShapeDtypeStruct((R, E), BF16),) * n,
        specs=[VP] * n + [VM] * (n + len(after)), flops=STEP_FLOPS, nbytes=12 * R * E,
    )(*own, *got, *after)


def back_kernel(
    scal_ref, ui_hbm, ni_hbm, ut_hbm, nt_hbm, dv_hbm, du_ref, qa_ref, qb_ref,
    di_ref, dt_ref, keep_ref, send_ref, ui_ref, ni_ref, ut_ref, nt_ref, dv_ref, sem,
):
    get = [
        pltpu.make_async_copy(src, dst, sem.at[k])
        for k, (src, dst) in enumerate(
            ((dv_hbm, dv_ref), (ui_hbm, ui_ref), (ni_hbm, ni_ref), (ut_hbm, ut_ref), (nt_hbm, nt_ref))
        )
    ]
    for c in get:
        c.start()
    scale = scal_ref[0, 0]
    low = scal_ref[0, 1] == 0.0
    du = scale * (du_ref[...].astype(F32) + qa_ref[...].astype(F32) + qb_ref[...].astype(F32))
    for c in get:
        c.wait()
    dv = dv_ref[:R].astype(F32)
    for j in range(1, 8):
        dv = dv + dv_ref[j * R : (j + 1) * R].astype(F32)
    dv = scale * dv
    for k, (unit_ref, norm_ref, grad, out_ref) in enumerate(
        ((ui_ref, ni_ref, du, di_ref), (ut_ref, nt_ref, dv, dt_ref))
    ):
        unit = unit_ref[...]
        d = (grad - unit * jnp.sum(unit * grad, axis=1, keepdims=True)) / norm_ref[:, :1]
        out_ref[...] = d.astype(BF16)
        left, right = d[:, :H], d[:, H:]
        keep_ref[k * R : (k + 1) * R] = jnp.where(low, left, right).astype(BF16)
        send_ref[k * R : (k + 1) * R] = jnp.where(low, right, left).astype(BF16)


def back(scal, *args):
    low = jax.ShapeDtypeStruct((R, E), BF16)
    half = jax.ShapeDtypeStruct((2 * R, H), BF16)
    return vmem_call(
        back_kernel, (low, low, half, half), specs=[SM] + [HB] * 5 + [VP] + [VM] * 2,
        scratch=(
            pltpu.VMEM((R, E), F32),
            pltpu.VMEM((R, 128), F32),
            pltpu.VMEM((R, E), F32),
            pltpu.VMEM((R, 128), F32),
            pltpu.VMEM((8 * R, E), BF16),
            pltpu.SemaphoreType.DMA((5,)),
        ),
        flops=20 * R * E, nbytes=30 * R * E,
    )(scal, *args)


def input_grad_kernel(di_ref, dt_ref, head_ref, gi_ref, gt_ref, done_ref):
    head = head_ref[...]
    done_ref[...] = jnp.zeros((8, 128), F32)
    gi_ref[...] = dot(di_ref[...], head, NT).astype(BF16)
    gt_ref[...] = dot(dt_ref[...], head, NT).astype(BF16)


def input_grad(di, dt, head):
    out = jax.ShapeDtypeStruct((R, D), BF16)
    return vmem_call(
        input_grad_kernel, (out, out, jax.ShapeDtypeStruct((8, 128), F32)), n_in=3, flops=4 * R * D * E, nbytes=2 * (4 * R * D + D * E)
    )(di, dt, head)


ZROWS = 24
PAD = 16


def turn_kernel(*refs):
    hbm, (out_ref, x_all, sem) = refs[:4], refs[-3:]
    get = []
    for i, src in enumerate(hbm):
        get.append(pltpu.make_async_copy(src, x_all.at[pl.ds(i * R, R)], sem.at[i]))
        get[i].start()
    for c in get:
        c.wait()
    out_ref[...] = x_all[...].T


def turn(*data):
    return vmem_call(
        turn_kernel, jax.ShapeDtypeStruct((D, 4 * R), BF16),
        scratch=(pltpu.VMEM((4 * R, D), BF16), pltpu.SemaphoreType.DMA((4,))),
        specs=[HB] * 4, out_specs=VP, flops=4 * R * D, nbytes=16 * R * D,
    )(*data)


def head_grad_kernel(xt_ref, keep_ref, got_ref, extra_ref, out_hbm, d_all, out_v, out_sem):
    d_all[: 2 * R] = keep_ref[...]
    d_all[2 * R :] = got_ref[...]
    for j in range(8):
        out_v[j, 8 * ZROWS :] = extra_ref[...]
    d = d_all[...]
    put = []
    for xl in range(2):
        full = dot(xt_ref[xl * E : (xl + 1) * E], d, NN)
        for y in range(4):
            for z in range(0, 8, 2):
                a = (z * 4 + y) * ZROWS
                b = ((z + 1) * 4 + y) * ZROWS
                both = jnp.concatenate([full[a : a + ZROWS], full[b : b + ZROWS]], axis=0)
                out_v[xl * 4 + y, z * ZROWS : (z + 2) * ZROWS] = both.astype(BF16)
        at = pl.ds(xl * 4, 4)
        put.append(pltpu.make_async_copy(out_v.at[at], out_hbm.at[at], out_sem.at[xl]))
        put[xl].start()
    for c in put:
        c.wait()


def head_grad_parts(xt, keep, got, extra):
    shape = (8, 8 * ZROWS + PAD, H)
    return vmem_call(
        head_grad_kernel, jax.ShapeDtypeStruct(shape, BF16),
        scratch=(
            pltpu.VMEM((4 * R, H), BF16),
            pltpu.VMEM(shape, BF16),
            pltpu.SemaphoreType.DMA((2,)),
        ),
        specs=[VP] + [VM] * 3, out_specs=HB, flops=8 * R * D * H, nbytes=2 * (4 * R * D + D * H),
    )(xt, keep, got, extra)


def sum_kernel(parts_ref, _, out_ref):
    s = parts_ref[0].astype(F32)
    for j in range(1, 8):
        s = s + parts_ref[j].astype(F32)
    t = jnp.sum(s[8 * ZROWS : 8 * ZROWS + 3], axis=0, keepdims=True)
    hi = t.astype(BF16).astype(F32)
    mid = (t - hi).astype(BF16).astype(F32)
    low = t - hi - mid
    row = lax.broadcasted_iota(jnp.int32, (8, H), 0)
    tail = jnp.where(row == 0, hi, jnp.where(row == 1, mid, jnp.where(row == 2, low, 0.0)))
    for z in range(8):
        out_ref[z] = jnp.concatenate([s[z * ZROWS : (z + 1) * ZROWS], tail], axis=0).astype(BF16)


def sum_parts(parts, after):
    return vmem_call(
        sum_kernel, jax.ShapeDtypeStruct((8, ZROWS + 8, H), BF16), n_in=2,
        flops=10 * parts.size, nbytes=2 * parts.size,
    )(parts, after)


def last_kernel(scal_ref, s_ref, r_ref, o_ref, hg_ref, l_ref, a_ref, b_ref):
    low = scal_ref[0, 1] == 0.0
    mine = s_ref[...] + r_ref[...]
    other = o_ref[...]
    left = jnp.where(low, mine, other)
    right = jnp.where(low, other, mine)
    hg_ref[:, :H] = left[:ZROWS]
    hg_ref[:, H:] = right[:ZROWS]
    t = jnp.sum((mine + other)[ZROWS : ZROWS + 3], axis=0, keepdims=True) * (1.0 / COUNT)
    l_ref[...] = t[:, 0:1]
    a_ref[...] = scal_ref[0, 0] * t[:, 1:2]
    b_ref[...] = t[:, 2:3]


COUNT = float(4 * 8192) * 8192.0


def last(scal, s, r, o):
    one = jax.ShapeDtypeStruct((1, 1), F32)
    return vmem_call(
        last_kernel, (jax.ShapeDtypeStruct((ZROWS, E), F32), one, one, one), smem=1, n_in=4,
        flops=ZROWS * E, nbytes=16 * ZROWS * E,
    )(scal, s, r, o)


def swap(axis):
    return lambda v: lax.ppermute(v, axis, [(0, 1), (1, 0)])


def ring(axis, n):
    even = [(i, i ^ 1) for i in range(n)]
    odd = [(i, (i + 1) % n if i % 2 else (i - 1) % n) for i in range(n)]
    return (lambda v: lax.ppermute(v, axis, even)), (lambda v: lax.ppermute(v, axis, odd))


def split3(t):
    hi = lax.reduce_precision(t, 8, 7)
    mid = lax.reduce_precision(t - hi, 8, 7)
    return hi, mid, t - hi - mid


def scalar_rows(t, rows):
    parts = jnp.stack(split3(t))
    return jnp.concatenate([parts, jnp.zeros((rows - 3, H), F32)]).astype(BF16)


def per_device(image, text, log_scale, bias, head):
    x = image[0]
    y = text[0]
    scale = jnp.exp(log_scale)
    core = lax.axis_index("c")
    z1, z2 = ring("z", 8)
    cc = swap("c")
    near = ("xl", "y")

    u, v, ui, ni, ut, nt = project(x, y, head)

    a1, b1 = z1(u), z2(u)
    vs = lax.all_to_all(v, near, 0, 0, tiled=True)
    a2, b2 = z1(b1), z2(a1)
    a3, b3 = z1(b2), z2(a2)
    far = z1(b3)
    xt = turn(x, y, cc(x), cc(y))

    scal = jnp.stack([scale * LOG2E, bias * LOG2E]).reshape(1, 2)
    at = (lax.axis_index(near) * R).reshape(1, 1)
    us = (u, a1, b1, a2, b2, a3, b3)
    p0, pa1, pb1, pa2, pb2, pa3, pb3, g1, sums = pair(((0,), (1, 2), (3, 4), (5, 6)), True, scal, at, vs, us)
    pf, g2, sums = pair(((0,),), False, scal, at, vs, (far,), (sums,))

    dv, done = pair_cols(g1, g2, (*us, far))
    (qa,) = ring_step((pb3,), (z1(pf),), (done,))
    dv = lax.all_to_all(dv, near, 0, 0, tiled=True)
    qa, qb = ring_step((pa2, pb2), (z2(qa), z1(pa3)))
    qa, qb = ring_step((pb1, pa1), (z1(qa), z2(qb)))
    qa, qb = z2(qa), z1(qb)

    sums = jnp.sum(sums, axis=(1, 2))
    extra = scalar_rows(jnp.zeros((H,), F32).at[:3].set(sums), PAD)

    scal2 = jnp.stack([scale, core.astype(F32)]).reshape(1, 2)
    di, dt, keep, send = back(scal2, ui, ni, ut, nt, dv, p0, qa, qb)
    got = cc(send)
    gi, gt, done = input_grad(di, dt, head)

    parts = head_grad_parts(xt, keep, got, extra)
    parts = lax.all_to_all(parts, ("xl", "y"), 0, 0, tiled=True)
    parts = lax.all_to_all(sum_parts(parts, done), "z", 0, 0, tiled=True)
    s = jnp.sum(parts.astype(F32), axis=0)
    r = swap("xh")(s)
    o = cc(s + r)
    hg, l, a, b = last(scal2, s, r, o)
    return l.reshape(()), a.reshape(()), b.reshape(()), gi[None], gt[None], hg


def solution(mesh):
    fine = Mesh(mesh.devices.reshape(2, 8, 4, 2, 2), ("xl", "z", "y", "xh", "c"))
    blk = ("xl", "z", "y")
    rep = ("xh", "c")
    data = P(rep, blk, None)
    return jax.shard_map(
        per_device,
        mesh=fine,
        in_specs=(data, data, P(), P(), P()),
        out_specs=(P(), P(), P(), data, data, P(blk, None)),
        check_vma=False,
    )
```

```python
import functools
import math

import jax
import jax.numpy as jnp
from jax import lax
from jax.experimental import pallas as pl
from jax.experimental.pallas import tpu as pltpu
from jax.sharding import Mesh, PartitionSpec as P

F32 = jnp.float32
BF16 = jnp.bfloat16
LOG2E = 1.4426950408889634
LN2 = 0.6931471805599453
R = 128
E = 768
D = 1536
H = E // 2

NT = (((1,), (1,)), ((), ()))
NN = (((1,), (0,)), ((), ()))
TN = (((0,), (0,)), ((), ()))


def dot(a, b, dims):
    return lax.dot_general(a, b, dims, preferred_element_type=F32)


GRANT = 6 << 20
VM = pl.BlockSpec(memory_space=pltpu.VMEM)
SM = pl.BlockSpec(memory_space=pltpu.SMEM)
HB = pl.BlockSpec(memory_space=pltpu.HBM)
VP = pl.BlockSpec(memory_space=pltpu.VMEM, index_map=None)


def vmem_call(kernel, out_shape, scratch=(), smem=0, n_in=0, flops=0, nbytes=0, specs=None, out_specs=None):
    if specs is None:
        specs = [SM] * smem + [VM] * (n_in - smem)
    if out_specs is None:
        out_specs = jax.tree.map(lambda _: VM, out_shape)

    def place_out(t, spec):
        if spec is HB:
            return pltpu.HBM(t.shape, t.dtype)
        if spec is VP:
            return pltpu.VMEM(t.shape, t.dtype)
        return t

    def place_in(t, spec):
        if spec is HB:
            return pltpu.with_memory_space_constraint(t, pltpu.HBM)
        if spec is VP:
            return pltpu.with_memory_space_constraint(t, pltpu.VMEM)
        return t

    def call(*args):
        held = sum(t.size * jnp.dtype(t.dtype).itemsize for t in (*args, *jax.tree.leaves(out_shape)))
        held += sum(4 * math.prod(t.shape) for t in scratch)
        return pl.pallas_call(
            kernel,
            out_shape=jax.tree.map(place_out, out_shape, out_specs),
            in_specs=specs,
            out_specs=out_specs,
            scratch_shapes=list(scratch),
            compiler_params=pltpu.CompilerParams(vmem_limit_bytes=2 * held + GRANT),
            cost_estimate=pl.CostEstimate(flops=flops, bytes_accessed=nbytes, transcendentals=0),
        )(*(place_in(t, spec) for t, spec in zip(args, specs)))

    return call


PARTS = 3


def proj_kernel(
    x_hbm, y_hbm, head_hbm, u_ref, v_hbm, ui_hbm, ni_hbm, ut_hbm, nt_hbm,
    x_v, y_v, head_v, unit_v, norm_v, low_v, in_sem, out_sem,
):
    deep = D // PARTS
    get_x = pltpu.make_async_copy(x_hbm, x_v, in_sem.at[PARTS])
    get_y = pltpu.make_async_copy(y_hbm, y_v, in_sem.at[PARTS + 1])
    get = [
        pltpu.make_async_copy(head_hbm.at[pl.ds(k * deep, deep)], head_v.at[pl.ds(k * deep, deep)], in_sem.at[k])
        for k in range(PARTS)
    ]
    get_y.start()
    for c in get:
        c.start()
    get_x.start()
    put = []

    def send(src, dst):
        put.append(pltpu.make_async_copy(src, dst, out_sem.at[len(put)]))
        put[-1].start()

    def finish(k, proj, unit_hbm, norm_hbm):
        norm = jnp.sqrt(jnp.sum(proj * proj, axis=1, keepdims=True) + 1e-06)
        unit = proj / norm
        unit_v[k] = unit
        norm_v[k] = jnp.broadcast_to(norm, (R, 128))
        send(unit_v.at[k], unit_hbm)
        send(norm_v.at[k], norm_hbm)
        return unit.astype(BF16)

    get_y.wait()
    proj = None
    for k, c in enumerate(get):
        c.wait()
        part = dot(y_v[:, k * deep : (k + 1) * deep], head_v[k * deep : (k + 1) * deep], NN)
        proj = part if proj is None else proj + part
    low_v[...] = finish(0, proj, ut_hbm, nt_hbm)
    for k in range(8):
        send(low_v, v_hbm.at[pl.ds(k * R, R)])
    get_x.wait()
    u_ref[...] = finish(1, dot(x_v[...], head_v[...], NN), ui_hbm, ni_hbm)
    for c in put:
        c.wait()


def project(x, y, head):
    unit = jax.ShapeDtypeStruct((R, E), F32)
    norm = jax.ShapeDtypeStruct((R, 128), F32)
    return vmem_call(
        proj_kernel,
        (jax.ShapeDtypeStruct((R, E), BF16), jax.ShapeDtypeStruct((8 * R, E), BF16), unit, norm, unit, norm),
        scratch=(
            pltpu.VMEM((R, D), BF16),
            pltpu.VMEM((R, D), BF16),
            pltpu.VMEM((D, E), BF16),
            pltpu.VMEM((2, R, E), F32),
            pltpu.VMEM((2, R, 128), F32),
            pltpu.VMEM((R, E), BF16),
            pltpu.SemaphoreType.DMA((PARTS + 2,)),
            pltpu.SemaphoreType.DMA((12,)),
        ),
        specs=[HB] * 3, out_specs=(VM, HB, HB, HB, HB, HB),
        flops=4 * R * D * E, nbytes=2 * (2 * R * D + D * E),
    )(x, y, head)


SUB = 8
CB = 256
RB = 32


def pair_elementwise(s_ref, g_ref, rows, scale2, bias2, diag_at):
    acc_m = jnp.zeros((SUB, CB), F32)
    acc_l = jnp.zeros((SUB, CB), F32)
    acc_s = jnp.zeros((SUB, CB), F32)
    acc_g = jnp.zeros((SUB, CB), F32)

    def fold(t):
        return jnp.sum(t.reshape(RB // SUB, SUB, CB), axis=0)

    for c in range(s_ref.shape[1] // CB):
        prod = jnp.ones((SUB, CB), F32)
        for r in range(rows // RB):
            s = s_ref[r * RB : (r + 1) * RB, c * CB : (c + 1) * CB]
            z = s * scale2 + bias2
            if diag_at is not None:
                row = r * RB + lax.broadcasted_iota(jnp.int32, (RB, CB), 0)
                col = c * CB + lax.broadcasted_iota(jnp.int32, (RB, CB), 1)
                mask = row + diag_at == col
                z = jnp.where(mask, -z, z)
            t = jnp.exp2(-jnp.abs(z))
            one_t = 1.0 + t
            inv = 1.0 / one_t
            g = jnp.where(z >= 0.0, inv, t * inv)
            if diag_at is not None:
                g = jnp.where(mask, -g, g)
            g_ref[r * RB : (r + 1) * RB, c * CB : (c + 1) * CB] = g.astype(BF16)
            acc_m = acc_m + fold(jnp.maximum(z, 0.0))
            acc_s = acc_s + fold(g * s)
            acc_g = acc_g + fold(g)
            for k in range(RB // SUB):
                prod = prod * one_t[k * SUB : (k + 1) * SUB]
        acc_l = acc_l + jnp.log(prod)
    return LN2 * acc_m + acc_l, acc_s, acc_g


def pair_kernel(chunks, own, scal_ref, at_ref, v_ref, *refs):
    n = sum(len(c) for c in chunks)
    if not own:
        before_ref, refs = refs[0], refs[1:]
    u_refs, du_refs, (g_ref, sums_ref, u_all, s_all) = refs[:n], refs[n : 2 * n], refs[2 * n :]
    scale2 = scal_ref[0, 0]
    bias2 = scal_ref[0, 1]
    v = v_ref[...]
    tot = None
    at = 0
    for i, chunk in enumerate(chunks):
        rows = 0
        for k in chunk:
            u_all[i % 2, rows : rows + u_refs[k].shape[0]] = u_refs[k][...]
            rows += u_refs[k].shape[0]
        s_all[i % 2, :rows] = dot(u_all[i % 2, :rows], v, NT)
        part = pair_elementwise(
            s_all.at[i % 2], g_ref.at[pl.ds(at, rows)], rows, scale2, bias2,
            at_ref[0, 0] if own and i == 0 else None,
        )
        tot = part if tot is None else tuple(a + b for a, b in zip(tot, part))
        du = dot(g_ref[at : at + rows], v, NN)
        at += rows
        rows = 0
        for k in chunk:
            ref = du_refs[k]
            ref[...] = du[rows : rows + ref.shape[0]].astype(ref.dtype)
            rows += ref.shape[0]
    for i in range(3):
        sums_ref[i] = tot[i] if own else tot[i] + before_ref[i]


def pair(chunks, own, scal, at, v, us, before=()):
    rows = sum(u.shape[0] for u in us)
    most = max(sum(us[k].shape[0] for k in c) for c in chunks)
    cols = v.shape[0]
    out = (
        *(jax.ShapeDtypeStruct(u.shape, BF16) for u in us),
        jax.ShapeDtypeStruct((rows, cols), BF16),
        jax.ShapeDtypeStruct((3, SUB, CB), F32),
    )
    return vmem_call(
        functools.partial(pair_kernel, chunks, own), out,
        scratch=(pltpu.VMEM((2, most, E), BF16), pltpu.VMEM((2, most, cols), F32)),
        specs=[SM, SM] + [VM] * (1 + len(before) + len(us)), out_specs=(VP,) * (len(us) + 2),
        flops=4 * rows * cols * E, nbytes=4 * (rows + cols) * E,
    )(scal, at, v, *before, *us)


def cols_kernel(n, *refs):
    g_refs, u_refs, (dv_hbm, done_ref, u_all, dv_ref, sem) = refs[:n], refs[n:-5], refs[-5:]
    done_ref[...] = jnp.zeros(done_ref.shape, F32)
    at = 0
    for ref in u_refs:
        u_all[at : at + R] = ref[...]
        at += R
    cols = dv_ref.shape[0] // 2
    put = []
    for i in range(2):
        at = pl.ds(i * cols, cols)
        dv = None
        row = 0
        for g in g_refs:
            k = g.shape[0]
            part = dot(g[:, at], u_all[row : row + k], TN)
            dv = part if dv is None else dv + part
            row += k
        dv_ref[at] = dv.astype(BF16)
        put.append(pltpu.make_async_copy(dv_ref.at[at], dv_hbm.at[at], sem.at[i]))
        put[i].start()
    for c in put:
        c.wait()


def pair_cols(gs, us):
    rows = sum(g.shape[0] for g in gs)
    cols = gs[0].shape[1]
    return vmem_call(
        functools.partial(cols_kernel, len(gs)),
        (jax.ShapeDtypeStruct((cols, E), BF16), jax.ShapeDtypeStruct((8, 128), F32)),
        scratch=(pltpu.VMEM((rows, E), BF16), pltpu.VMEM((cols, E), BF16), pltpu.SemaphoreType.DMA((2,))),
        specs=[VP] * len(gs) + [VM] * len(us), out_specs=(HB, VM),
        flops=2 * rows * cols * E, nbytes=2 * (rows * cols + rows * E + cols * E),
    )(*gs, *us)


def step_kernel(n, *refs):
    for k in range(n):
        refs[-n + k][...] = (refs[k][...].astype(F32) + refs[n + k][...].astype(F32)).astype(BF16)


STEP_FLOPS = 8 * 10**9


def ring_step(own, got, after=()):
    n = len(own)
    return vmem_call(
        functools.partial(step_kernel, n), (jax.ShapeDtypeStruct((R, E), BF16),) * n,
        specs=[VP] * n + [VM] * (n + len(after)), flops=STEP_FLOPS, nbytes=12 * R * E,
    )(*own, *got, *after)


def back_kernel(
    scal_ref, ui_hbm, ni_hbm, ut_hbm, nt_hbm, dv_hbm, du_ref, qa_ref, qb_ref,
    di_ref, dt_ref, keep_ref, send_ref, ui_ref, ni_ref, ut_ref, nt_ref, dv_ref, sem,
):
    get = [
        pltpu.make_async_copy(src, dst, sem.at[k])
        for k, (src, dst) in enumerate(
            ((ui_hbm, ui_ref), (ni_hbm, ni_ref), (ut_hbm, ut_ref), (nt_hbm, nt_ref), (dv_hbm, dv_ref))
        )
    ]
    for c in get:
        c.start()
    scale = scal_ref[0, 0]
    low = scal_ref[0, 1] == 0.0

    def finish(k, unit_ref, norm_ref, grad, out_ref):
        unit = unit_ref[...]
        d = (grad - unit * jnp.sum(unit * grad, axis=1, keepdims=True)) / norm_ref[:, :1]
        out_ref[...] = d.astype(BF16)
        left, right = d[:, :H], d[:, H:]
        keep_ref[k * R : (k + 1) * R] = jnp.where(low, left, right).astype(BF16)
        send_ref[k * R : (k + 1) * R] = jnp.where(low, right, left).astype(BF16)

    du = scale * (du_ref[...].astype(F32) + qa_ref[...].astype(F32) + qb_ref[...].astype(F32))
    get[0].wait()
    get[1].wait()
    finish(0, ui_ref, ni_ref, du, di_ref)
    for c in get[2:]:
        c.wait()
    dv = dv_ref[:R].astype(F32)
    for j in range(1, 8):
        dv = dv + dv_ref[j * R : (j + 1) * R].astype(F32)
    finish(1, ut_ref, nt_ref, scale * dv, dt_ref)


def back(scal, *args):
    low = jax.ShapeDtypeStruct((R, E), BF16)
    half = jax.ShapeDtypeStruct((2 * R, H), BF16)
    return vmem_call(
        back_kernel, (low, low, half, half), specs=[SM] + [HB] * 5 + [VP] + [VM] * 2,
        scratch=(
            pltpu.VMEM((R, E), F32),
            pltpu.VMEM((R, 128), F32),
            pltpu.VMEM((R, E), F32),
            pltpu.VMEM((R, 128), F32),
            pltpu.VMEM((8 * R, E), BF16),
            pltpu.SemaphoreType.DMA((5,)),
        ),
        flops=20 * R * E, nbytes=30 * R * E,
    )(scal, *args)


def input_grad_kernel(di_ref, dt_ref, head_ref, gi_ref, gt_ref, done_ref):
    head = head_ref[...]
    done_ref[...] = jnp.zeros((8, 128), F32)
    gi_ref[...] = dot(di_ref[...], head, NT).astype(BF16)
    gt_ref[...] = dot(dt_ref[...], head, NT).astype(BF16)


def input_grad(di, dt, head):
    out = jax.ShapeDtypeStruct((R, D), BF16)
    return vmem_call(
        input_grad_kernel, (out, out, jax.ShapeDtypeStruct((8, 128), F32)), n_in=3, flops=4 * R * D * E, nbytes=2 * (4 * R * D + D * E)
    )(di, dt, head)


ZROWS = 24
PAD = 16


def turn_kernel(*refs):
    hbm, (out_ref, x_all, sem) = refs[:4], refs[-3:]
    get = []
    for i, src in enumerate(hbm):
        get.append(pltpu.make_async_copy(src, x_all.at[pl.ds(i * R, R)], sem.at[i]))
        get[i].start()
    for c in get:
        c.wait()
    out_ref[...] = x_all[...].T


def turn(*data):
    return vmem_call(
        turn_kernel, jax.ShapeDtypeStruct((D, 4 * R), BF16),
        scratch=(pltpu.VMEM((4 * R, D), BF16), pltpu.SemaphoreType.DMA((4,))),
        specs=[HB] * 4, out_specs=VP, flops=4 * R * D, nbytes=16 * R * D,
    )(*data)


def head_grad_kernel(xt_ref, keep_ref, got_ref, extra_ref, out_hbm, d_all, out_v, out_sem):
    d_all[: 2 * R] = keep_ref[...]
    d_all[2 * R :] = got_ref[...]
    for j in range(8):
        out_v[j, 8 * ZROWS :] = extra_ref[...]
    d = d_all[...]
    put = []
    for xl in range(2):
        full = dot(xt_ref[xl * E : (xl + 1) * E], d, NN)
        for y in range(4):
            for z in range(0, 8, 2):
                a = (z * 4 + y) * ZROWS
                b = ((z + 1) * 4 + y) * ZROWS
                both = jnp.concatenate([full[a : a + ZROWS], full[b : b + ZROWS]], axis=0)
                out_v[xl * 4 + y, z * ZROWS : (z + 2) * ZROWS] = both.astype(BF16)
        at = pl.ds(xl * 4, 4)
        put.append(pltpu.make_async_copy(out_v.at[at], out_hbm.at[at], out_sem.at[xl]))
        put[xl].start()
    for c in put:
        c.wait()


def head_grad_parts(xt, keep, got, extra):
    shape = (8, 8 * ZROWS + PAD, H)
    return vmem_call(
        head_grad_kernel, jax.ShapeDtypeStruct(shape, BF16),
        scratch=(
            pltpu.VMEM((4 * R, H), BF16),
            pltpu.VMEM(shape, BF16),
            pltpu.SemaphoreType.DMA((2,)),
        ),
        specs=[VP] + [VM] * 3, out_specs=HB, flops=8 * R * D * H, nbytes=2 * (4 * R * D + D * H),
    )(xt, keep, got, extra)


def sum_kernel(parts_hbm, _, out_ref, parts_v, sem):
    get = [pltpu.make_async_copy(parts_hbm.at[j], parts_v.at[j], sem.at[j]) for j in range(8)]
    for c in get:
        c.start()
    s = None
    for j in range(0, 8, 2):
        get[j].wait()
        get[j + 1].wait()
        pair_sum = parts_v[j].astype(F32) + parts_v[j + 1].astype(F32)
        s = pair_sum if s is None else s + pair_sum
    t = jnp.sum(s[8 * ZROWS : 8 * ZROWS + 3], axis=0, keepdims=True)
    hi = t.astype(BF16).astype(F32)
    mid = (t - hi).astype(BF16).astype(F32)
    low = t - hi - mid
    row = lax.broadcasted_iota(jnp.int32, (8, H), 0)
    tail = jnp.where(row == 0, hi, jnp.where(row == 1, mid, jnp.where(row == 2, low, 0.0)))
    for z in range(8):
        out_ref[z] = jnp.concatenate([s[z * ZROWS : (z + 1) * ZROWS], tail], axis=0).astype(BF16)


def sum_parts(parts, after):
    return vmem_call(
        sum_kernel, jax.ShapeDtypeStruct((8, ZROWS + 8, H), BF16), specs=[HB, VM],
        scratch=(pltpu.VMEM(parts.shape, BF16), pltpu.SemaphoreType.DMA((8,))),
        flops=10 * parts.size, nbytes=2 * parts.size,
    )(parts, after)


def last_kernel(scal_ref, s_ref, r_ref, o_ref, hg_ref, l_ref, a_ref, b_ref):
    low = scal_ref[0, 1] == 0.0
    mine = s_ref[...] + r_ref[...]
    other = o_ref[...]
    left = jnp.where(low, mine, other)
    right = jnp.where(low, other, mine)
    hg_ref[:, :H] = left[:ZROWS]
    hg_ref[:, H:] = right[:ZROWS]
    t = jnp.sum((mine + other)[ZROWS : ZROWS + 3], axis=0, keepdims=True) * (1.0 / COUNT)
    l_ref[...] = t[:, 0:1]
    a_ref[...] = scal_ref[0, 0] * t[:, 1:2]
    b_ref[...] = t[:, 2:3]


COUNT = float(4 * 8192) * 8192.0


def last(scal, s, r, o):
    one = jax.ShapeDtypeStruct((1, 1), F32)
    return vmem_call(
        last_kernel, (jax.ShapeDtypeStruct((ZROWS, E), F32), one, one, one), smem=1, n_in=4,
        flops=ZROWS * E, nbytes=16 * ZROWS * E,
    )(scal, s, r, o)


def swap(axis):
    return lambda v: lax.ppermute(v, axis, [(0, 1), (1, 0)])


def ring(axis, n):
    even = [(i, i ^ 1) for i in range(n)]
    odd = [(i, (i + 1) % n if i % 2 else (i - 1) % n) for i in range(n)]
    return (lambda v: lax.ppermute(v, axis, even)), (lambda v: lax.ppermute(v, axis, odd))


def split3(t):
    hi = lax.reduce_precision(t, 8, 7)
    mid = lax.reduce_precision(t - hi, 8, 7)
    return hi, mid, t - hi - mid


def scalar_rows(t, rows):
    parts = jnp.stack(split3(t))
    return jnp.concatenate([parts, jnp.zeros((rows - 3, H), F32)]).astype(BF16)


def per_device(image, text, log_scale, bias, head):
    x = image[0]
    y = text[0]
    scale = jnp.exp(log_scale)
    core = lax.axis_index("c")
    z1, z2 = ring("z", 8)
    cc = swap("c")
    near = ("xl", "y")

    u, v, ui, ni, ut, nt = project(x, y, head)

    a1, b1 = z1(u), z2(u)
    vs = lax.all_to_all(v, near, 0, 0, tiled=True)
    a2, b2 = z1(b1), z2(a1)
    a3, b3 = z1(b2), z2(a2)
    far = z1(b3)
    xt = turn(x, y, cc(x), cc(y))

    scal = jnp.stack([scale * LOG2E, bias * LOG2E]).reshape(1, 2)
    at = (lax.axis_index(near) * R).reshape(1, 1)
    us = (u, a1, b1, a2, b2, a3, b3)
    p0, pa1, pb1, pa2, pb2, g1, sums = pair(((0,), (1, 2), (3, 4)), True, scal, at, vs, us[:5])
    pa3, pb3, g2, sums = pair(((0, 1),), False, scal, at, vs, us[5:], (sums,))
    pf, g3, sums = pair(((0,),), False, scal, at, vs, (far,), (sums,))

    dv, done = pair_cols((g1, g2, g3), (*us, far))
    (qa,) = ring_step((pb3,), (z1(pf),), (done,))
    dv = lax.all_to_all(dv, near, 0, 0, tiled=True)
    qa, qb = ring_step((pa2, pb2), (z2(qa), z1(pa3)))
    qa, qb = ring_step((pb1, pa1), (z1(qa), z2(qb)))
    qa, qb = z2(qa), z1(qb)

    sums = jnp.sum(sums, axis=(1, 2))
    extra = scalar_rows(jnp.zeros((H,), F32).at[:3].set(sums), PAD)

    scal2 = jnp.stack([scale, core.astype(F32)]).reshape(1, 2)
    di, dt, keep, send = back(scal2, ui, ni, ut, nt, dv, p0, qa, qb)
    got = cc(send)
    gi, gt, done = input_grad(di, dt, head)

    parts = head_grad_parts(xt, keep, got, extra)
    parts = lax.all_to_all(parts, ("xl", "y"), 0, 0, tiled=True)
    parts = lax.all_to_all(sum_parts(parts, done), "z", 0, 0, tiled=True)
    s = jnp.sum(parts.astype(F32), axis=0)
    r = swap("xh")(s)
    o = cc(s + r)
    hg, l, a, b = last(scal2, s, r, o)
    return l.reshape(()), a.reshape(()), b.reshape(()), gi[None], gt[None], hg


def solution(mesh):
    fine = Mesh(mesh.devices.reshape(2, 8, 4, 2, 2), ("xl", "z", "y", "xh", "c"))
    blk = ("xl", "z", "y")
    rep = ("xh", "c")
    data = P(rep, blk, None)
    return jax.shard_map(
        per_device,
        mesh=fine,
        in_specs=(data, data, P(), P(), P()),
        out_specs=(P(), P(), P(), data, data, P(blk, None)),
        check_vma=False,
    )
```

```python
import functools
import math

import jax
import jax.numpy as jnp
from jax import lax
from jax.experimental import pallas as pl
from jax.experimental.pallas import tpu as pltpu
from jax.sharding import Mesh, PartitionSpec as P

F32 = jnp.float32
BF16 = jnp.bfloat16
LOG2E = 1.4426950408889634
LN2 = 0.6931471805599453
R = 128
E = 768
D = 1536
H = E // 2

NT = (((1,), (1,)), ((), ()))
NN = (((1,), (0,)), ((), ()))
TN = (((0,), (0,)), ((), ()))


def dot(a, b, dims):
    return lax.dot_general(a, b, dims, preferred_element_type=F32)


GRANT = 6 << 20
VM = pl.BlockSpec(memory_space=pltpu.VMEM)
SM = pl.BlockSpec(memory_space=pltpu.SMEM)
HB = pl.BlockSpec(memory_space=pltpu.HBM)
VP = pl.BlockSpec(memory_space=pltpu.VMEM, index_map=None)


def vmem_call(kernel, out_shape, scratch=(), smem=0, n_in=0, flops=0, nbytes=0, specs=None, out_specs=None):
    if specs is None:
        specs = [SM] * smem + [VM] * (n_in - smem)
    if out_specs is None:
        out_specs = jax.tree.map(lambda _: VM, out_shape)

    def place_out(t, spec):
        if spec is HB:
            return pltpu.HBM(t.shape, t.dtype)
        if spec is VP:
            return pltpu.VMEM(t.shape, t.dtype)
        return t

    def place_in(t, spec):
        if spec is HB:
            return pltpu.with_memory_space_constraint(t, pltpu.HBM)
        if spec is VP:
            return pltpu.with_memory_space_constraint(t, pltpu.VMEM)
        return t

    def call(*args):
        held = sum(t.size * jnp.dtype(t.dtype).itemsize for t in (*args, *jax.tree.leaves(out_shape)))
        held += sum(4 * math.prod(t.shape) for t in scratch)
        return pl.pallas_call(
            kernel,
            out_shape=jax.tree.map(place_out, out_shape, out_specs),
            in_specs=specs,
            out_specs=out_specs,
            scratch_shapes=list(scratch),
            compiler_params=pltpu.CompilerParams(vmem_limit_bytes=2 * held + GRANT),
            cost_estimate=pl.CostEstimate(flops=flops, bytes_accessed=nbytes, transcendentals=0),
        )(*(place_in(t, spec) for t, spec in zip(args, specs)))

    return call


PARTS = 3


def proj_kernel(
    x_hbm, y_hbm, head_hbm, u_ref, v_hbm, ui_hbm, ni_hbm, ut_hbm, nt_hbm,
    x_v, y_v, head_v, unit_v, norm_v, low_v, in_sem, out_sem,
):
    deep = D // PARTS
    get_x = pltpu.make_async_copy(x_hbm, x_v, in_sem.at[PARTS])
    get_y = pltpu.make_async_copy(y_hbm, y_v, in_sem.at[PARTS + 1])
    get = [
        pltpu.make_async_copy(head_hbm.at[pl.ds(k * deep, deep)], head_v.at[pl.ds(k * deep, deep)], in_sem.at[k])
        for k in range(PARTS)
    ]
    get_y.start()
    for c in get:
        c.start()
    get_x.start()
    put = []

    def send(src, dst):
        put.append(pltpu.make_async_copy(src, dst, out_sem.at[len(put)]))
        put[-1].start()

    def finish(k, proj, unit_hbm, norm_hbm):
        norm = jnp.sqrt(jnp.sum(proj * proj, axis=1, keepdims=True) + 1e-06)
        unit = proj / norm
        unit_v[k] = unit
        norm_v[k] = jnp.broadcast_to(norm, (R, 128))
        send(unit_v.at[k], unit_hbm)
        send(norm_v.at[k], norm_hbm)
        return unit.astype(BF16)

    get_y.wait()
    proj = None
    for k, c in enumerate(get):
        c.wait()
        part = dot(y_v[:, k * deep : (k + 1) * deep], head_v[k * deep : (k + 1) * deep], NN)
        proj = part if proj is None else proj + part
    low_v[...] = finish(0, proj, ut_hbm, nt_hbm)
    for k in range(8):
        send(low_v, v_hbm.at[pl.ds(k * R, R)])
    get_x.wait()
    u_ref[...] = finish(1, dot(x_v[...], head_v[...], NN), ui_hbm, ni_hbm)
    for c in put:
        c.wait()


def project(x, y, head):
    unit = jax.ShapeDtypeStruct((R, E), F32)
    norm = jax.ShapeDtypeStruct((R, 128), F32)
    return vmem_call(
        proj_kernel,
        (jax.ShapeDtypeStruct((R, E), BF16), jax.ShapeDtypeStruct((8 * R, E), BF16), unit, norm, unit, norm),
        scratch=(
            pltpu.VMEM((R, D), BF16),
            pltpu.VMEM((R, D), BF16),
            pltpu.VMEM((D, E), BF16),
            pltpu.VMEM((2, R, E), F32),
            pltpu.VMEM((2, R, 128), F32),
            pltpu.VMEM((R, E), BF16),
            pltpu.SemaphoreType.DMA((PARTS + 2,)),
            pltpu.SemaphoreType.DMA((12,)),
        ),
        specs=[HB] * 3, out_specs=(VM, HB, HB, HB, HB, HB),
        flops=4 * R * D * E, nbytes=2 * (2 * R * D + D * E),
    )(x, y, head)


SUB = 8
CB = 256
RB = 32


def pair_elementwise(s_ref, g_ref, rows, scale2, bias2, diag_at):
    acc_m = jnp.zeros((SUB, CB), F32)
    acc_l = jnp.zeros((SUB, CB), F32)
    acc_s = jnp.zeros((SUB, CB), F32)
    acc_g = jnp.zeros((SUB, CB), F32)

    def fold(t):
        return jnp.sum(t.reshape(RB // SUB, SUB, CB), axis=0)

    for c in range(s_ref.shape[1] // CB):
        prod = jnp.ones((SUB, CB), F32)
        for r in range(rows // RB):
            s = s_ref[r * RB : (r + 1) * RB, c * CB : (c + 1) * CB]
            z = s * scale2 + bias2
            if diag_at is not None:
                row = r * RB + lax.broadcasted_iota(jnp.int32, (RB, CB), 0)
                col = c * CB + lax.broadcasted_iota(jnp.int32, (RB, CB), 1)
                mask = row + diag_at == col
                z = jnp.where(mask, -z, z)
            t = jnp.exp2(-jnp.abs(z))
            one_t = 1.0 + t
            inv = 1.0 / one_t
            g = jnp.where(z >= 0.0, inv, t * inv)
            if diag_at is not None:
                g = jnp.where(mask, -g, g)
            g_ref[r * RB : (r + 1) * RB, c * CB : (c + 1) * CB] = g.astype(BF16)
            acc_m = acc_m + fold(jnp.maximum(z, 0.0))
            acc_s = acc_s + fold(g * s)
            acc_g = acc_g + fold(g)
            for k in range(RB // SUB):
                prod = prod * one_t[k * SUB : (k + 1) * SUB]
        acc_l = acc_l + jnp.log(prod)
    return LN2 * acc_m + acc_l, acc_s, acc_g


def pair_kernel(chunks, own, scal_ref, at_ref, v_ref, *refs):
    n = sum(len(c) for c in chunks)
    if not own:
        before_ref, refs = refs[0], refs[1:]
    u_refs, du_refs, (g_ref, sums_ref, u_all, s_all) = refs[:n], refs[n : 2 * n], refs[2 * n :]
    scale2 = scal_ref[0, 0]
    bias2 = scal_ref[0, 1]
    v = v_ref[...]
    tot = None
    at = 0
    for i, chunk in enumerate(chunks):
        rows = 0
        for k in chunk:
            u_all[i % 2, rows : rows + u_refs[k].shape[0]] = u_refs[k][...]
            rows += u_refs[k].shape[0]
        s_all[i % 2, :rows] = dot(u_all[i % 2, :rows], v, NT)
        part = pair_elementwise(
            s_all.at[i % 2], g_ref.at[pl.ds(at, rows)], rows, scale2, bias2,
            at_ref[0, 0] if own and i == 0 else None,
        )
        tot = part if tot is None else tuple(a + b for a, b in zip(tot, part))
        du = dot(g_ref[at : at + rows], v, NN)
        at += rows
        rows = 0
        for k in chunk:
            ref = du_refs[k]
            ref[...] = du[rows : rows + ref.shape[0]].astype(ref.dtype)
            rows += ref.shape[0]
    for i in range(3):
        sums_ref[i] = tot[i] if own else tot[i] + before_ref[i]


def pair(chunks, own, scal, at, v, us, before=()):
    rows = sum(u.shape[0] for u in us)
    most = max(sum(us[k].shape[0] for k in c) for c in chunks)
    cols = v.shape[0]
    out = (
        *(jax.ShapeDtypeStruct(u.shape, BF16) for u in us),
        jax.ShapeDtypeStruct((rows, cols), BF16),
        jax.ShapeDtypeStruct((3, SUB, CB), F32),
    )
    return vmem_call(
        functools.partial(pair_kernel, chunks, own), out,
        scratch=(pltpu.VMEM((2, most, E), BF16), pltpu.VMEM((2, most, cols), F32)),
        specs=[SM, SM] + [VM] * (1 + len(before) + len(us)), out_specs=(VP,) * (len(us) + 2),
        flops=4 * rows * cols * E, nbytes=4 * (rows + cols) * E,
    )(scal, at, v, *before, *us)


def cols_kernel(n, *refs):
    g_refs, u_refs, (dv_hbm, done_ref, u_all, dv_ref, sem) = refs[:n], refs[n:-5], refs[-5:]
    done_ref[...] = jnp.zeros(done_ref.shape, F32)
    at = 0
    for ref in u_refs:
        u_all[at : at + R] = ref[...]
        at += R
    cols = dv_ref.shape[0] // 2
    put = []
    for i in range(2):
        at = pl.ds(i * cols, cols)
        dv = None
        row = 0
        for g in g_refs:
            k = g.shape[0]
            part = dot(g[:, at], u_all[row : row + k], TN)
            dv = part if dv is None else dv + part
            row += k
        dv_ref[at] = dv.astype(BF16)
        put.append(pltpu.make_async_copy(dv_ref.at[at], dv_hbm.at[at], sem.at[i]))
        put[i].start()
    for c in put:
        c.wait()


def pair_cols(gs, us):
    rows = sum(g.shape[0] for g in gs)
    cols = gs[0].shape[1]
    return vmem_call(
        functools.partial(cols_kernel, len(gs)),
        (jax.ShapeDtypeStruct((cols, E), BF16), jax.ShapeDtypeStruct((8, 128), F32)),
        scratch=(pltpu.VMEM((rows, E), BF16), pltpu.VMEM((cols, E), BF16), pltpu.SemaphoreType.DMA((2,))),
        specs=[VP] * len(gs) + [VM] * len(us), out_specs=(HB, VM),
        flops=2 * rows * cols * E, nbytes=2 * (rows * cols + rows * E + cols * E),
    )(*gs, *us)


def step_kernel(n, *refs):
    for k in range(n):
        refs[-n + k][...] = (refs[k][...].astype(F32) + refs[n + k][...].astype(F32)).astype(BF16)


STEP_FLOPS = 8 * 10**9


def ring_step(own, got, after=()):
    n = len(own)
    return vmem_call(
        functools.partial(step_kernel, n), (jax.ShapeDtypeStruct((R, E), BF16),) * n,
        specs=[VP] * n + [VM] * (n + len(after)), flops=STEP_FLOPS, nbytes=12 * R * E,
    )(*own, *got, *after)


def back_kernel(
    scal_ref, ui_hbm, ni_hbm, ut_hbm, nt_hbm, dv_hbm, du_ref, qa_ref, qb_ref,
    di_ref, dt_ref, keep_ref, send_ref, ui_ref, ni_ref, ut_ref, nt_ref, dv_ref, sem,
):
    get = [
        pltpu.make_async_copy(src, dst, sem.at[k])
        for k, (src, dst) in enumerate(
            ((ui_hbm, ui_ref), (ni_hbm, ni_ref), (ut_hbm, ut_ref), (nt_hbm, nt_ref), (dv_hbm, dv_ref))
        )
    ]
    for c in get:
        c.start()
    scale = scal_ref[0, 0]
    low = scal_ref[0, 1] == 0.0

    def finish(k, unit_ref, norm_ref, grad, out_ref):
        unit = unit_ref[...]
        d = (grad - unit * jnp.sum(unit * grad, axis=1, keepdims=True)) / norm_ref[:, :1]
        out_ref[...] = d.astype(BF16)
        left, right = d[:, :H], d[:, H:]
        keep_ref[k * R : (k + 1) * R] = jnp.where(low, left, right).astype(BF16)
        send_ref[k * R : (k + 1) * R] = jnp.where(low, right, left).astype(BF16)

    du = scale * (du_ref[...].astype(F32) + qa_ref[...].astype(F32) + qb_ref[...].astype(F32))
    get[0].wait()
    get[1].wait()
    finish(0, ui_ref, ni_ref, du, di_ref)
    for c in get[2:]:
        c.wait()
    dv = dv_ref[:R].astype(F32)
    for j in range(1, 8):
        dv = dv + dv_ref[j * R : (j + 1) * R].astype(F32)
    finish(1, ut_ref, nt_ref, scale * dv, dt_ref)


def back(scal, *args):
    low = jax.ShapeDtypeStruct((R, E), BF16)
    half = jax.ShapeDtypeStruct((2 * R, H), BF16)
    return vmem_call(
        back_kernel, (low, low, half, half), specs=[SM] + [HB] * 5 + [VP] + [VM] * 2,
        scratch=(
            pltpu.VMEM((R, E), F32),
            pltpu.VMEM((R, 128), F32),
            pltpu.VMEM((R, E), F32),
            pltpu.VMEM((R, 128), F32),
            pltpu.VMEM((8 * R, E), BF16),
            pltpu.SemaphoreType.DMA((5,)),
        ),
        flops=20 * R * E, nbytes=30 * R * E,
    )(scal, *args)


def input_grad_kernel(di_ref, dt_ref, head_ref, gi_ref, gt_ref, done_ref):
    head = head_ref[...]
    done_ref[...] = jnp.zeros((8, 128), F32)
    gi_ref[...] = dot(di_ref[...], head, NT).astype(BF16)
    gt_ref[...] = dot(dt_ref[...], head, NT).astype(BF16)


def input_grad(di, dt, head):
    out = jax.ShapeDtypeStruct((R, D), BF16)
    return vmem_call(
        input_grad_kernel, (out, out, jax.ShapeDtypeStruct((8, 128), F32)), n_in=3, flops=4 * R * D * E, nbytes=2 * (4 * R * D + D * E)
    )(di, dt, head)


ZROWS = 24
PAD = 16


def turn_kernel(*refs):
    hbm, (out_ref, x_all, sem) = refs[:4], refs[-3:]
    get = []
    for i, src in enumerate(hbm):
        get.append(pltpu.make_async_copy(src, x_all.at[pl.ds(i * R, R)], sem.at[i]))
        get[i].start()
    for c in get:
        c.wait()
    out_ref[...] = x_all[...].T


def turn(*data):
    return vmem_call(
        turn_kernel, jax.ShapeDtypeStruct((D, 4 * R), BF16),
        scratch=(pltpu.VMEM((4 * R, D), BF16), pltpu.SemaphoreType.DMA((4,))),
        specs=[HB] * 4, out_specs=VP, flops=4 * R * D, nbytes=16 * R * D,
    )(*data)


def own_head_kernel(xt_ref, keep_ref, out_ref):
    out_ref[...] = dot(xt_ref[:, : 2 * R], keep_ref[...], NN)


def own_head(xt, keep):
    return vmem_call(
        own_head_kernel, jax.ShapeDtypeStruct((D, H), F32), specs=[VP, VM], out_specs=VP,
        flops=4 * R * D * H, nbytes=4 * R * D + 4 * D * H,
    )(xt, keep)


def head_grad_kernel(xt_ref, own_ref, got_ref, extra_ref, out_hbm, out_v, out_sem):
    for j in range(8):
        out_v[j, 8 * ZROWS :] = extra_ref[...]
    d = got_ref[...]
    put = []
    for xl in range(2):
        rows = slice(xl * E, (xl + 1) * E)
        full = own_ref[rows] + dot(xt_ref[rows, 2 * R :], d, NN)
        for y in range(4):
            for z in range(0, 8, 2):
                a = (z * 4 + y) * ZROWS
                b = ((z + 1) * 4 + y) * ZROWS
                both = jnp.concatenate([full[a : a + ZROWS], full[b : b + ZROWS]], axis=0)
                out_v[xl * 4 + y, z * ZROWS : (z + 2) * ZROWS] = both.astype(BF16)
        at = pl.ds(xl * 4, 4)
        put.append(pltpu.make_async_copy(out_v.at[at], out_hbm.at[at], out_sem.at[xl]))
        put[xl].start()
    for c in put:
        c.wait()


def head_grad_parts(xt, own, got, extra):
    shape = (8, 8 * ZROWS + PAD, H)
    return vmem_call(
        head_grad_kernel, jax.ShapeDtypeStruct(shape, BF16),
        scratch=(pltpu.VMEM(shape, BF16), pltpu.SemaphoreType.DMA((2,))),
        specs=[VP, VP, VM, VM], out_specs=HB, flops=4 * R * D * H, nbytes=2 * (4 * R * D + D * H),
    )(xt, own, got, extra)


def sum_kernel(parts_hbm, _, out_ref, parts_v, sem):
    get = [pltpu.make_async_copy(parts_hbm.at[j], parts_v.at[j], sem.at[j]) for j in range(8)]
    for c in get:
        c.start()
    s = None
    for j in range(0, 8, 2):
        get[j].wait()
        get[j + 1].wait()
        pair_sum = parts_v[j].astype(F32) + parts_v[j + 1].astype(F32)
        s = pair_sum if s is None else s + pair_sum
    t = jnp.sum(s[8 * ZROWS : 8 * ZROWS + 3], axis=0, keepdims=True)
    hi = t.astype(BF16).astype(F32)
    mid = (t - hi).astype(BF16).astype(F32)
    low = t - hi - mid
    row = lax.broadcasted_iota(jnp.int32, (8, H), 0)
    tail = jnp.where(row == 0, hi, jnp.where(row == 1, mid, jnp.where(row == 2, low, 0.0)))
    for z in range(8):
        out_ref[z] = jnp.concatenate([s[z * ZROWS : (z + 1) * ZROWS], tail], axis=0).astype(BF16)


def sum_parts(parts, after):
    return vmem_call(
        sum_kernel, jax.ShapeDtypeStruct((8, ZROWS + 8, H), BF16), specs=[HB, VM],
        scratch=(pltpu.VMEM(parts.shape, BF16), pltpu.SemaphoreType.DMA((8,))),
        flops=10 * parts.size, nbytes=2 * parts.size,
    )(parts, after)


def last_kernel(scal_ref, s_ref, r_ref, o_ref, hg_ref, l_ref, a_ref, b_ref):
    low = scal_ref[0, 1] == 0.0
    mine = s_ref[...] + r_ref[...]
    other = o_ref[...]
    left = jnp.where(low, mine, other)
    right = jnp.where(low, other, mine)
    hg_ref[:, :H] = left[:ZROWS]
    hg_ref[:, H:] = right[:ZROWS]
    t = jnp.sum((mine + other)[ZROWS : ZROWS + 3], axis=0, keepdims=True) * (1.0 / COUNT)
    l_ref[...] = t[:, 0:1]
    a_ref[...] = scal_ref[0, 0] * t[:, 1:2]
    b_ref[...] = t[:, 2:3]


COUNT = float(4 * 8192) * 8192.0


def last(scal, s, r, o):
    one = jax.ShapeDtypeStruct((1, 1), F32)
    return vmem_call(
        last_kernel, (jax.ShapeDtypeStruct((ZROWS, E), F32), one, one, one), smem=1, n_in=4,
        flops=ZROWS * E, nbytes=16 * ZROWS * E,
    )(scal, s, r, o)


def swap(axis):
    return lambda v: lax.ppermute(v, axis, [(0, 1), (1, 0)])


def ring(axis, n):
    even = [(i, i ^ 1) for i in range(n)]
    odd = [(i, (i + 1) % n if i % 2 else (i - 1) % n) for i in range(n)]
    return (lambda v: lax.ppermute(v, axis, even)), (lambda v: lax.ppermute(v, axis, odd))


def split3(t):
    hi = lax.reduce_precision(t, 8, 7)
    mid = lax.reduce_precision(t - hi, 8, 7)
    return hi, mid, t - hi - mid


def scalar_rows(t, rows):
    parts = jnp.stack(split3(t))
    return jnp.concatenate([parts, jnp.zeros((rows - 3, H), F32)]).astype(BF16)


def per_device(image, text, log_scale, bias, head):
    x = image[0]
    y = text[0]
    scale = jnp.exp(log_scale)
    core = lax.axis_index("c")
    z1, z2 = ring("z", 8)
    cc = swap("c")
    near = ("xl", "y")

    u, v, ui, ni, ut, nt = project(x, y, head)

    a1, b1 = z1(u), z2(u)
    vs = lax.all_to_all(v, near, 0, 0, tiled=True)
    a2, b2 = z1(b1), z2(a1)
    a3, b3 = z1(b2), z2(a2)
    far = z1(b3)
    xt = turn(x, y, cc(x), cc(y))

    scal = jnp.stack([scale * LOG2E, bias * LOG2E]).reshape(1, 2)
    at = (lax.axis_index(near) * R).reshape(1, 1)
    us = (u, a1, b1, a2, b2, a3, b3)
    p0, pa1, pb1, pa2, pb2, g1, sums = pair(((0,), (1, 2), (3, 4)), True, scal, at, vs, us[:5])
    pa3, pb3, g2, sums = pair(((0, 1),), False, scal, at, vs, us[5:], (sums,))
    pf, g3, sums = pair(((0,),), False, scal, at, vs, (far,), (sums,))

    dv, done = pair_cols((g1, g2, g3), (*us, far))
    (qa,) = ring_step((pb3,), (z1(pf),), (done,))
    dv = lax.all_to_all(dv, near, 0, 0, tiled=True)
    qa, qb = ring_step((pa2, pb2), (z2(qa), z1(pa3)))
    qa, qb = ring_step((pb1, pa1), (z1(qa), z2(qb)))
    qa, qb = z2(qa), z1(qb)

    sums = jnp.sum(sums, axis=(1, 2))
    extra = scalar_rows(jnp.zeros((H,), F32).at[:3].set(sums), PAD)

    scal2 = jnp.stack([scale, core.astype(F32)]).reshape(1, 2)
    di, dt, keep, send = back(scal2, ui, ni, ut, nt, dv, p0, qa, qb)
    got = cc(send)
    gi, gt, done = input_grad(di, dt, head)

    parts = head_grad_parts(xt, own_head(xt, keep), got, extra)
    parts = lax.all_to_all(parts, ("xl", "y"), 0, 0, tiled=True)
    parts = lax.all_to_all(sum_parts(parts, done), "z", 0, 0, tiled=True)
    s = jnp.sum(parts.astype(F32), axis=0)
    r = swap("xh")(s)
    o = cc(s + r)
    hg, l, a, b = last(scal2, s, r, o)
    return l.reshape(()), a.reshape(()), b.reshape(()), gi[None], gt[None], hg


def solution(mesh):
    fine = Mesh(mesh.devices.reshape(2, 8, 4, 2, 2), ("xl", "z", "y", "xh", "c"))
    blk = ("xl", "z", "y")
    rep = ("xh", "c")
    data = P(rep, blk, None)
    return jax.shard_map(
        per_device,
        mesh=fine,
        in_specs=(data, data, P(), P(), P()),
        out_specs=(P(), P(), P(), data, data, P(blk, None)),
        check_vma=False,
    )
```

```python
import functools
import math

import jax
import jax.numpy as jnp
from jax import lax
from jax.experimental import pallas as pl
from jax.experimental.pallas import tpu as pltpu
from jax.sharding import Mesh, PartitionSpec as P

F32 = jnp.float32
BF16 = jnp.bfloat16
LOG2E = 1.4426950408889634
LN2 = 0.6931471805599453
R = 128
E = 768
D = 1536
H = E // 2

NT = (((1,), (1,)), ((), ()))
NN = (((1,), (0,)), ((), ()))
TN = (((0,), (0,)), ((), ()))


def dot(a, b, dims):
    return lax.dot_general(a, b, dims, preferred_element_type=F32)


GRANT = 6 << 20
VM = pl.BlockSpec(memory_space=pltpu.VMEM)
SM = pl.BlockSpec(memory_space=pltpu.SMEM)
HB = pl.BlockSpec(memory_space=pltpu.HBM)
VP = pl.BlockSpec(memory_space=pltpu.VMEM, index_map=None)


def vmem_call(kernel, out_shape, scratch=(), smem=0, n_in=0, flops=0, nbytes=0, specs=None, out_specs=None):
    if specs is None:
        specs = [SM] * smem + [VM] * (n_in - smem)
    if out_specs is None:
        out_specs = jax.tree.map(lambda _: VM, out_shape)

    def place_out(t, spec):
        if spec is HB:
            return pltpu.HBM(t.shape, t.dtype)
        if spec is VP:
            return pltpu.VMEM(t.shape, t.dtype)
        return t

    def place_in(t, spec):
        if spec is HB:
            return pltpu.with_memory_space_constraint(t, pltpu.HBM)
        if spec is VP:
            return pltpu.with_memory_space_constraint(t, pltpu.VMEM)
        return t

    def call(*args):
        held = sum(t.size * jnp.dtype(t.dtype).itemsize for t in (*args, *jax.tree.leaves(out_shape)))
        held += sum(4 * math.prod(t.shape) for t in scratch)
        return pl.pallas_call(
            kernel,
            out_shape=jax.tree.map(place_out, out_shape, out_specs),
            in_specs=specs,
            out_specs=out_specs,
            scratch_shapes=list(scratch),
            compiler_params=pltpu.CompilerParams(vmem_limit_bytes=2 * held + GRANT),
            cost_estimate=pl.CostEstimate(flops=flops, bytes_accessed=nbytes, transcendentals=0),
        )(*(place_in(t, spec) for t, spec in zip(args, specs)))

    return call


PARTS = 6


def proj_kernel(
    x_hbm, y_hbm, head_hbm, u_ref, v_hbm, ui_hbm, ni_hbm, ut_hbm, nt_hbm,
    xy_v, head_v, unit_v, norm_v, low_v, in_sem, out_sem,
):
    deep = D // PARTS
    get = [
        pltpu.make_async_copy(y_hbm, xy_v.at[pl.ds(0, R)], in_sem.at[PARTS]),
        pltpu.make_async_copy(x_hbm, xy_v.at[pl.ds(R, R)], in_sem.at[PARTS + 1]),
    ] + [
        pltpu.make_async_copy(head_hbm.at[pl.ds(k * deep, deep)], head_v.at[pl.ds(k * deep, deep)], in_sem.at[k])
        for k in range(PARTS)
    ]
    for c in get:
        c.start()
    put = []

    def send(src, dst):
        put.append(pltpu.make_async_copy(src, dst, out_sem.at[len(put)]))
        put[-1].start()

    def finish(k, proj, unit_hbm, norm_hbm):
        norm = jnp.sqrt(jnp.sum(proj * proj, axis=1, keepdims=True) + 1e-06)
        unit = proj / norm
        unit_v[k] = unit
        norm_v[k] = jnp.broadcast_to(norm, (R, 128))
        send(unit_v.at[k], unit_hbm)
        send(norm_v.at[k], norm_hbm)
        return unit.astype(BF16)

    get[0].wait()
    get[1].wait()
    proj = None
    for k in range(PARTS):
        get[2 + k].wait()
        part = dot(xy_v[:, k * deep : (k + 1) * deep], head_v[k * deep : (k + 1) * deep], NN)
        proj = part if proj is None else proj + part
    low_v[...] = finish(0, proj[:R], ut_hbm, nt_hbm)
    for k in range(8):
        send(low_v, v_hbm.at[pl.ds(k * R, R)])
    u_ref[...] = finish(1, proj[R:], ui_hbm, ni_hbm)
    for c in put:
        c.wait()


def project(x, y, head):
    unit = jax.ShapeDtypeStruct((R, E), F32)
    norm = jax.ShapeDtypeStruct((R, 128), F32)
    return vmem_call(
        proj_kernel,
        (jax.ShapeDtypeStruct((R, E), BF16), jax.ShapeDtypeStruct((8 * R, E), BF16), unit, norm, unit, norm),
        scratch=(
            pltpu.VMEM((2 * R, D), BF16),
            pltpu.VMEM((D, E), BF16),
            pltpu.VMEM((2, R, E), F32),
            pltpu.VMEM((2, R, 128), F32),
            pltpu.VMEM((R, E), BF16),
            pltpu.SemaphoreType.DMA((PARTS + 2,)),
            pltpu.SemaphoreType.DMA((12,)),
        ),
        specs=[HB] * 3, out_specs=(VM, HB, HB, HB, HB, HB),
        flops=4 * R * D * E, nbytes=2 * (2 * R * D + D * E),
    )(x, y, head)


SUB = 8
CB = 256
RB = 32


def pair_elementwise(s_ref, g_ref, rows, scale2, bias2, diag_at):
    acc_m = jnp.zeros((SUB, CB), F32)
    acc_l = jnp.zeros((SUB, CB), F32)
    acc_s = jnp.zeros((SUB, CB), F32)
    acc_g = jnp.zeros((SUB, CB), F32)

    def fold(t):
        return jnp.sum(t.reshape(RB // SUB, SUB, CB), axis=0)

    for c in range(s_ref.shape[1] // CB):
        prod = jnp.ones((SUB, CB), F32)
        for r in range(rows // RB):
            s = s_ref[r * RB : (r + 1) * RB, c * CB : (c + 1) * CB]
            z = s * scale2 + bias2
            if diag_at is not None:
                row = r * RB + lax.broadcasted_iota(jnp.int32, (RB, CB), 0)
                col = c * CB + lax.broadcasted_iota(jnp.int32, (RB, CB), 1)
                mask = row + diag_at == col
                z = jnp.where(mask, -z, z)
            t = jnp.exp2(-jnp.abs(z))
            one_t = 1.0 + t
            inv = 1.0 / one_t
            g = jnp.where(z >= 0.0, inv, t * inv)
            if diag_at is not None:
                g = jnp.where(mask, -g, g)
            g_ref[r * RB : (r + 1) * RB, c * CB : (c + 1) * CB] = g.astype(BF16)
            acc_m = acc_m + fold(jnp.maximum(z, 0.0))
            acc_s = acc_s + fold(g * s)
            acc_g = acc_g + fold(g)
            for k in range(RB // SUB):
                prod = prod * one_t[k * SUB : (k + 1) * SUB]
        acc_l = acc_l + jnp.log(prod)
    return LN2 * acc_m + acc_l, acc_s, acc_g


def pair_kernel(chunks, own, scal_ref, at_ref, v_ref, *refs):
    n = sum(len(c) for c in chunks)
    if not own:
        before_ref, refs = refs[0], refs[1:]
    u_refs, du_refs, (g_ref, sums_ref, u_all, s_all) = refs[:n], refs[n : 2 * n], refs[2 * n :]
    scale2 = scal_ref[0, 0]
    bias2 = scal_ref[0, 1]
    v = v_ref[...]
    tot = None
    at = 0
    for i, chunk in enumerate(chunks):
        rows = 0
        for k in chunk:
            u_all[i % 2, rows : rows + u_refs[k].shape[0]] = u_refs[k][...]
            rows += u_refs[k].shape[0]
        s_all[i % 2, :rows] = dot(u_all[i % 2, :rows], v, NT)
        part = pair_elementwise(
            s_all.at[i % 2], g_ref.at[pl.ds(at, rows)], rows, scale2, bias2,
            at_ref[0, 0] if own and i == 0 else None,
        )
        tot = part if tot is None else tuple(a + b for a, b in zip(tot, part))
        du = dot(g_ref[at : at + rows], v, NN)
        at += rows
        rows = 0
        for k in chunk:
            ref = du_refs[k]
            ref[...] = du[rows : rows + ref.shape[0]].astype(ref.dtype)
            rows += ref.shape[0]
    for i in range(3):
        sums_ref[i] = tot[i] if own else tot[i] + before_ref[i]


def pair(chunks, own, scal, at, v, us, before=()):
    rows = sum(u.shape[0] for u in us)
    most = max(sum(us[k].shape[0] for k in c) for c in chunks)
    cols = v.shape[0]
    out = (
        *(jax.ShapeDtypeStruct(u.shape, BF16) for u in us),
        jax.ShapeDtypeStruct((rows, cols), BF16),
        jax.ShapeDtypeStruct((3, SUB, CB), F32),
    )
    return vmem_call(
        functools.partial(pair_kernel, chunks, own), out,
        scratch=(pltpu.VMEM((2, most, E), BF16), pltpu.VMEM((2, most, cols), F32)),
        specs=[SM, SM] + [VM] * (1 + len(before) + len(us)), out_specs=(VP,) * (len(us) + 2),
        flops=4 * rows * cols * E, nbytes=4 * (rows + cols) * E,
    )(scal, at, v, *before, *us)


def cols_kernel(n, *refs):
    g_refs, u_refs, (dv_hbm, done_ref, u_all, dv_ref, sem) = refs[:n], refs[n:-5], refs[-5:]
    done_ref[...] = jnp.zeros(done_ref.shape, F32)
    at = 0
    for ref in u_refs:
        u_all[at : at + R] = ref[...]
        at += R
    cols = dv_ref.shape[0] // 2
    put = []
    for i in range(2):
        at = pl.ds(i * cols, cols)
        dv = None
        row = 0
        for g in g_refs:
            k = g.shape[0]
            part = dot(g[:, at], u_all[row : row + k], TN)
            dv = part if dv is None else dv + part
            row += k
        dv_ref[at] = dv.astype(BF16)
        put.append(pltpu.make_async_copy(dv_ref.at[at], dv_hbm.at[at], sem.at[i]))
        put[i].start()
    for c in put:
        c.wait()


def pair_cols(gs, us):
    rows = sum(g.shape[0] for g in gs)
    cols = gs[0].shape[1]
    return vmem_call(
        functools.partial(cols_kernel, len(gs)),
        (jax.ShapeDtypeStruct((cols, E), BF16), jax.ShapeDtypeStruct((8, 128), F32)),
        scratch=(pltpu.VMEM((rows, E), BF16), pltpu.VMEM((cols, E), BF16), pltpu.SemaphoreType.DMA((2,))),
        specs=[VP] * len(gs) + [VM] * len(us), out_specs=(HB, VM),
        flops=2 * rows * cols * E, nbytes=2 * (rows * cols + rows * E + cols * E),
    )(*gs, *us)


def step_kernel(n, *refs):
    for k in range(n):
        refs[-n + k][...] = (refs[k][...].astype(F32) + refs[n + k][...].astype(F32)).astype(BF16)


STEP_FLOPS = 8 * 10**9


def ring_step(own, got, after=()):
    n = len(own)
    return vmem_call(
        functools.partial(step_kernel, n), (jax.ShapeDtypeStruct((R, E), BF16),) * n,
        specs=[VP] * n + [VM] * (n + len(after)), flops=STEP_FLOPS, nbytes=12 * R * E,
    )(*own, *got, *after)


def back_kernel(
    scal_ref, ui_hbm, ni_hbm, ut_hbm, nt_hbm, dv_hbm, du_ref, qa_ref, qb_ref,
    di_ref, dt_ref, keep_ref, send_ref, ui_ref, ni_ref, ut_ref, nt_ref, dv_ref, sem,
):
    get = [
        pltpu.make_async_copy(src, dst, sem.at[k])
        for k, (src, dst) in enumerate(
            ((ui_hbm, ui_ref), (ni_hbm, ni_ref), (ut_hbm, ut_ref), (nt_hbm, nt_ref), (dv_hbm, dv_ref))
        )
    ]
    for c in get:
        c.start()
    scale = scal_ref[0, 0]
    low = scal_ref[0, 1] == 0.0

    def finish(k, unit_ref, norm_ref, grad, out_ref):
        unit = unit_ref[...]
        d = (grad - unit * jnp.sum(unit * grad, axis=1, keepdims=True)) / norm_ref[:, :1]
        out_ref[...] = d.astype(BF16)
        left, right = d[:, :H], d[:, H:]
        keep_ref[k * R : (k + 1) * R] = jnp.where(low, left, right).astype(BF16)
        send_ref[k * R : (k + 1) * R] = jnp.where(low, right, left).astype(BF16)

    du = scale * (du_ref[...].astype(F32) + qa_ref[...].astype(F32) + qb_ref[...].astype(F32))
    get[0].wait()
    get[1].wait()
    finish(0, ui_ref, ni_ref, du, di_ref)
    for c in get[2:]:
        c.wait()
    dv = dv_ref[:R].astype(F32)
    for j in range(1, 8):
        dv = dv + dv_ref[j * R : (j + 1) * R].astype(F32)
    finish(1, ut_ref, nt_ref, scale * dv, dt_ref)


def back(scal, *args):
    low = jax.ShapeDtypeStruct((R, E), BF16)
    half = jax.ShapeDtypeStruct((2 * R, H), BF16)
    return vmem_call(
        back_kernel, (low, low, half, half), specs=[SM] + [HB] * 5 + [VP] + [VM] * 2,
        scratch=(
            pltpu.VMEM((R, E), F32),
            pltpu.VMEM((R, 128), F32),
            pltpu.VMEM((R, E), F32),
            pltpu.VMEM((R, 128), F32),
            pltpu.VMEM((8 * R, E), BF16),
            pltpu.SemaphoreType.DMA((5,)),
        ),
        flops=20 * R * E, nbytes=30 * R * E,
    )(scal, *args)


def input_grad_kernel(di_ref, dt_ref, head_ref, gi_ref, gt_ref, done_ref):
    head = head_ref[...]
    done_ref[...] = jnp.zeros((8, 128), F32)
    gi_ref[...] = dot(di_ref[...], head, NT).astype(BF16)
    gt_ref[...] = dot(dt_ref[...], head, NT).astype(BF16)


def input_grad(di, dt, head):
    out = jax.ShapeDtypeStruct((R, D), BF16)
    return vmem_call(
        input_grad_kernel, (out, out, jax.ShapeDtypeStruct((8, 128), F32)), n_in=3, flops=4 * R * D * E, nbytes=2 * (4 * R * D + D * E)
    )(di, dt, head)


ZROWS = 24
PAD = 16


def turn_kernel(*refs):
    hbm, (out_ref, x_all, sem) = refs[:4], refs[-3:]
    get = []
    for i, src in enumerate(hbm):
        get.append(pltpu.make_async_copy(src, x_all.at[pl.ds(i * R, R)], sem.at[i]))
        get[i].start()
    for c in get:
        c.wait()
    out_ref[...] = x_all[...].T


def turn(*data):
    return vmem_call(
        turn_kernel, jax.ShapeDtypeStruct((D, 4 * R), BF16),
        scratch=(pltpu.VMEM((4 * R, D), BF16), pltpu.SemaphoreType.DMA((4,))),
        specs=[HB] * 4, out_specs=VP, flops=4 * R * D, nbytes=16 * R * D,
    )(*data)


def own_head_kernel(xt_ref, keep_ref, out_ref):
    out_ref[...] = dot(xt_ref[:, : 2 * R], keep_ref[...], NN)


def own_head(xt, keep):
    return vmem_call(
        own_head_kernel, jax.ShapeDtypeStruct((D, H), F32), specs=[VP, VM], out_specs=VP,
        flops=4 * R * D * H, nbytes=4 * R * D + 4 * D * H,
    )(xt, keep)


def head_grad_kernel(xt_ref, own_ref, got_ref, extra_ref, out_hbm, out_v, out_sem):
    for j in range(8):
        out_v[j, 8 * ZROWS :] = extra_ref[...]
    d = got_ref[...]
    put = []
    for xl in range(2):
        rows = slice(xl * E, (xl + 1) * E)
        full = own_ref[rows] + dot(xt_ref[rows, 2 * R :], d, NN)
        for y in range(4):
            for z in range(0, 8, 2):
                a = (z * 4 + y) * ZROWS
                b = ((z + 1) * 4 + y) * ZROWS
                both = jnp.concatenate([full[a : a + ZROWS], full[b : b + ZROWS]], axis=0)
                out_v[xl * 4 + y, z * ZROWS : (z + 2) * ZROWS] = both.astype(BF16)
        at = pl.ds(xl * 4, 4)
        put.append(pltpu.make_async_copy(out_v.at[at], out_hbm.at[at], out_sem.at[xl]))
        put[xl].start()
    for c in put:
        c.wait()


def head_grad_parts(xt, own, got, extra):
    shape = (8, 8 * ZROWS + PAD, H)
    return vmem_call(
        head_grad_kernel, jax.ShapeDtypeStruct(shape, BF16),
        scratch=(pltpu.VMEM(shape, BF16), pltpu.SemaphoreType.DMA((2,))),
        specs=[VP, VP, VM, VM], out_specs=HB, flops=4 * R * D * H, nbytes=2 * (4 * R * D + D * H),
    )(xt, own, got, extra)


def sum_kernel(parts_hbm, _, out_ref, parts_v, sem):
    get = [pltpu.make_async_copy(parts_hbm.at[j], parts_v.at[j], sem.at[j]) for j in range(8)]
    for c in get:
        c.start()
    s = None
    for j in range(0, 8, 2):
        get[j].wait()
        get[j + 1].wait()
        pair_sum = parts_v[j].astype(F32) + parts_v[j + 1].astype(F32)
        s = pair_sum if s is None else s + pair_sum
    t = jnp.sum(s[8 * ZROWS : 8 * ZROWS + 3], axis=0, keepdims=True)
    hi = t.astype(BF16).astype(F32)
    mid = (t - hi).astype(BF16).astype(F32)
    low = t - hi - mid
    row = lax.broadcasted_iota(jnp.int32, (8, H), 0)
    tail = jnp.where(row == 0, hi, jnp.where(row == 1, mid, jnp.where(row == 2, low, 0.0)))
    for z in range(8):
        out_ref[z] = jnp.concatenate([s[z * ZROWS : (z + 1) * ZROWS], tail], axis=0).astype(BF16)


def sum_parts(parts, after):
    return vmem_call(
        sum_kernel, jax.ShapeDtypeStruct((8, ZROWS + 8, H), BF16), specs=[HB, VM],
        scratch=(pltpu.VMEM(parts.shape, BF16), pltpu.SemaphoreType.DMA((8,))),
        flops=10 * parts.size, nbytes=2 * parts.size,
    )(parts, after)


def last_kernel(scal_ref, s_ref, r_ref, o_ref, hg_ref, l_ref, a_ref, b_ref):
    low = scal_ref[0, 1] == 0.0
    mine = s_ref[...] + r_ref[...]
    other = o_ref[...]
    left = jnp.where(low, mine, other)
    right = jnp.where(low, other, mine)
    hg_ref[:, :H] = left[:ZROWS]
    hg_ref[:, H:] = right[:ZROWS]
    t = jnp.sum((mine + other)[ZROWS : ZROWS + 3], axis=0, keepdims=True) * (1.0 / COUNT)
    l_ref[...] = t[:, 0:1]
    a_ref[...] = scal_ref[0, 0] * t[:, 1:2]
    b_ref[...] = t[:, 2:3]


COUNT = float(4 * 8192) * 8192.0


def last(scal, s, r, o):
    one = jax.ShapeDtypeStruct((1, 1), F32)
    return vmem_call(
        last_kernel, (jax.ShapeDtypeStruct((ZROWS, E), F32), one, one, one), smem=1, n_in=4,
        flops=ZROWS * E, nbytes=16 * ZROWS * E,
    )(scal, s, r, o)


def swap(axis):
    return lambda v: lax.ppermute(v, axis, [(0, 1), (1, 0)])


def ring(axis, n):
    even = [(i, i ^ 1) for i in range(n)]
    odd = [(i, (i + 1) % n if i % 2 else (i - 1) % n) for i in range(n)]
    return (lambda v: lax.ppermute(v, axis, even)), (lambda v: lax.ppermute(v, axis, odd))


def split3(t):
    hi = lax.reduce_precision(t, 8, 7)
    mid = lax.reduce_precision(t - hi, 8, 7)
    return hi, mid, t - hi - mid


def scalar_rows(t, rows):
    parts = jnp.stack(split3(t))
    return jnp.concatenate([parts, jnp.zeros((rows - 3, H), F32)]).astype(BF16)


def per_device(image, text, log_scale, bias, head):
    x = image[0]
    y = text[0]
    scale = jnp.exp(log_scale)
    core = lax.axis_index("c")
    z1, z2 = ring("z", 8)
    cc = swap("c")
    near = ("xl", "y")

    u, v, ui, ni, ut, nt = project(x, y, head)

    a1, b1 = z1(u), z2(u)
    vs = lax.all_to_all(v, near, 0, 0, tiled=True)
    a2, b2 = z1(b1), z2(a1)
    a3, b3 = z1(b2), z2(a2)
    far = z1(b3)
    xt = turn(x, y, cc(x), cc(y))

    scal = jnp.stack([scale * LOG2E, bias * LOG2E]).reshape(1, 2)
    at = (lax.axis_index(near) * R).reshape(1, 1)
    us = (u, a1, b1, a2, b2, a3, b3)
    p0, pa1, pb1, pa2, pb2, g1, sums = pair(((0,), (1, 2), (3, 4)), True, scal, at, vs, us[:5])
    pa3, pb3, g2, sums = pair(((0, 1),), False, scal, at, vs, us[5:], (sums,))
    pf, g3, sums = pair(((0,),), False, scal, at, vs, (far,), (sums,))

    dv, done = pair_cols((g1, g2, g3), (*us, far))
    (qa,) = ring_step((pb3,), (z1(pf),), (done,))
    dv = lax.all_to_all(dv, near, 0, 0, tiled=True)
    qa, qb = ring_step((pa2, pb2), (z2(qa), z1(pa3)))
    qa, qb = ring_step((pb1, pa1), (z1(qa), z2(qb)))
    qa, qb = z2(qa), z1(qb)

    sums = jnp.sum(sums, axis=(1, 2))
    extra = scalar_rows(jnp.zeros((H,), F32).at[:3].set(sums), PAD)

    scal2 = jnp.stack([scale, core.astype(F32)]).reshape(1, 2)
    di, dt, keep, send = back(scal2, ui, ni, ut, nt, dv, p0, qa, qb)
    got = cc(send)
    gi, gt, done = input_grad(di, dt, head)

    parts = head_grad_parts(xt, own_head(xt, keep), got, extra)
    parts = lax.all_to_all(parts, ("xl", "y"), 0, 0, tiled=True)
    parts = lax.all_to_all(sum_parts(parts, done), "z", 0, 0, tiled=True)
    s = jnp.sum(parts.astype(F32), axis=0)
    r = swap("xh")(s)
    o = cc(s + r)
    hg, l, a, b = last(scal2, s, r, o)
    return l.reshape(()), a.reshape(()), b.reshape(()), gi[None], gt[None], hg


def solution(mesh):
    fine = Mesh(mesh.devices.reshape(2, 8, 4, 2, 2), ("xl", "z", "y", "xh", "c"))
    blk = ("xl", "z", "y")
    rep = ("xh", "c")
    data = P(rep, blk, None)
    return jax.shard_map(
        per_device,
        mesh=fine,
        in_specs=(data, data, P(), P(), P()),
        out_specs=(P(), P(), P(), data, data, P(blk, None)),
        check_vma=False,
    )
```

```python
import functools
import math

import jax
import jax.numpy as jnp
from jax import lax
from jax.experimental import pallas as pl
from jax.experimental.pallas import tpu as pltpu
from jax.sharding import Mesh, PartitionSpec as P

F32 = jnp.float32
BF16 = jnp.bfloat16
LOG2E = 1.4426950408889634
LN2 = 0.6931471805599453
R = 128
E = 768
D = 1536
H = E // 2

NT = (((1,), (1,)), ((), ()))
NN = (((1,), (0,)), ((), ()))
TN = (((0,), (0,)), ((), ()))


def dot(a, b, dims):
    return lax.dot_general(a, b, dims, preferred_element_type=F32)


GRANT = 6 << 20
VM = pl.BlockSpec(memory_space=pltpu.VMEM)
SM = pl.BlockSpec(memory_space=pltpu.SMEM)
HB = pl.BlockSpec(memory_space=pltpu.HBM)
VP = pl.BlockSpec(memory_space=pltpu.VMEM, index_map=None)


def vmem_call(kernel, out_shape, scratch=(), smem=0, n_in=0, flops=0, nbytes=0, specs=None, out_specs=None):
    if specs is None:
        specs = [SM] * smem + [VM] * (n_in - smem)
    if out_specs is None:
        out_specs = jax.tree.map(lambda _: VM, out_shape)

    def place_out(t, spec):
        if spec is HB:
            return pltpu.HBM(t.shape, t.dtype)
        if spec is VP:
            return pltpu.VMEM(t.shape, t.dtype)
        return t

    def place_in(t, spec):
        if spec is HB:
            return pltpu.with_memory_space_constraint(t, pltpu.HBM)
        if spec is VP:
            return pltpu.with_memory_space_constraint(t, pltpu.VMEM)
        return t

    def call(*args):
        held = sum(t.size * jnp.dtype(t.dtype).itemsize for t in (*args, *jax.tree.leaves(out_shape)))
        held += sum(4 * math.prod(t.shape) for t in scratch)
        return pl.pallas_call(
            kernel,
            out_shape=jax.tree.map(place_out, out_shape, out_specs),
            in_specs=specs,
            out_specs=out_specs,
            scratch_shapes=list(scratch),
            compiler_params=pltpu.CompilerParams(vmem_limit_bytes=2 * held + GRANT),
            cost_estimate=pl.CostEstimate(flops=flops, bytes_accessed=nbytes, transcendentals=0),
        )(*(place_in(t, spec) for t, spec in zip(args, specs)))

    return call


PARTS = 3


def proj_kernel(
    x_hbm, y_hbm, head_hbm, u_ref, v_hbm, ui_hbm, ni_hbm, ut_hbm, nt_hbm,
    x_v, y_v, head_v, unit_v, norm_v, low_v, in_sem, out_sem,
):
    deep = D // PARTS
    get_x = pltpu.make_async_copy(x_hbm, x_v, in_sem.at[PARTS])
    get_y = pltpu.make_async_copy(y_hbm, y_v, in_sem.at[PARTS + 1])
    get = [
        pltpu.make_async_copy(head_hbm.at[pl.ds(k * deep, deep)], head_v.at[pl.ds(k * deep, deep)], in_sem.at[k])
        for k in range(PARTS)
    ]
    get_y.start()
    for c in get:
        c.start()
    get_x.start()
    put = []

    def send(src, dst):
        put.append(pltpu.make_async_copy(src, dst, out_sem.at[len(put)]))
        put[-1].start()

    def finish(k, proj, unit_hbm, norm_hbm):
        norm = jnp.sqrt(jnp.sum(proj * proj, axis=1, keepdims=True) + 1e-06)
        unit = proj / norm
        unit_v[k] = unit
        norm_v[k] = jnp.broadcast_to(norm, (R, 128))
        send(unit_v.at[k], unit_hbm)
        send(norm_v.at[k], norm_hbm)
        return unit.astype(BF16)

    get_y.wait()
    proj = None
    for k, c in enumerate(get):
        c.wait()
        part = dot(y_v[:, k * deep : (k + 1) * deep], head_v[k * deep : (k + 1) * deep], NN)
        proj = part if proj is None else proj + part
    low_v[...] = finish(0, proj, ut_hbm, nt_hbm)
    for k in range(8):
        send(low_v, v_hbm.at[pl.ds(k * R, R)])
    get_x.wait()
    u_ref[...] = finish(1, dot(x_v[...], head_v[...], NN), ui_hbm, ni_hbm)
    for c in put:
        c.wait()


def project(x, y, head):
    unit = jax.ShapeDtypeStruct((R, E), F32)
    norm = jax.ShapeDtypeStruct((R, 128), F32)
    return vmem_call(
        proj_kernel,
        (jax.ShapeDtypeStruct((R, E), BF16), jax.ShapeDtypeStruct((8 * R, E), BF16), unit, norm, unit, norm),
        scratch=(
            pltpu.VMEM((R, D), BF16),
            pltpu.VMEM((R, D), BF16),
            pltpu.VMEM((D, E), BF16),
            pltpu.VMEM((2, R, E), F32),
            pltpu.VMEM((2, R, 128), F32),
            pltpu.VMEM((R, E), BF16),
            pltpu.SemaphoreType.DMA((PARTS + 2,)),
            pltpu.SemaphoreType.DMA((12,)),
        ),
        specs=[HB] * 3, out_specs=(VM, HB, HB, HB, HB, HB),
        flops=4 * R * D * E, nbytes=2 * (2 * R * D + D * E),
    )(x, y, head)


SUB = 8
CB = 256
RB = 32


def pair_elementwise(s_ref, g_ref, rows, scale2, bias2, diag_at):
    acc_m = jnp.zeros((SUB, CB), F32)
    acc_l = jnp.zeros((SUB, CB), F32)
    acc_s = jnp.zeros((SUB, CB), F32)
    acc_g = jnp.zeros((SUB, CB), F32)

    def fold(t):
        return jnp.sum(t.reshape(RB // SUB, SUB, CB), axis=0)

    for c in range(s_ref.shape[1] // CB):
        prod = jnp.ones((SUB, CB), F32)
        for r in range(rows // RB):
            s = s_ref[r * RB : (r + 1) * RB, c * CB : (c + 1) * CB]
            z = s * scale2 + bias2
            diag = diag_at is not None and r * RB < R
            if diag:
                row = r * RB + lax.broadcasted_iota(jnp.int32, (RB, CB), 0)
                col = c * CB + lax.broadcasted_iota(jnp.int32, (RB, CB), 1)
                mask = row + diag_at == col
                z = jnp.where(mask, -z, z)
            t = jnp.exp2(-jnp.abs(z))
            one_t = 1.0 + t
            inv = 1.0 / one_t
            g = jnp.where(z >= 0.0, inv, t * inv)
            if diag:
                g = jnp.where(mask, -g, g)
            g_ref[r * RB : (r + 1) * RB, c * CB : (c + 1) * CB] = g.astype(BF16)
            acc_m = acc_m + fold(jnp.maximum(z, 0.0))
            acc_s = acc_s + fold(g * s)
            acc_g = acc_g + fold(g)
            for k in range(RB // SUB):
                prod = prod * one_t[k * SUB : (k + 1) * SUB]
        acc_l = acc_l + jnp.log(prod)
    return LN2 * acc_m + acc_l, acc_s, acc_g


def pair_kernel(chunks, own, scal_ref, at_ref, v_ref, *refs):
    n = sum(len(c) for c in chunks)
    if not own:
        before_ref, refs = refs[0], refs[1:]
    u_refs, du_refs, (g_ref, sums_ref, u_all, s_all) = refs[:n], refs[n : 2 * n], refs[2 * n :]
    scale2 = scal_ref[0, 0]
    bias2 = scal_ref[0, 1]
    v = v_ref[...]
    tot = None
    at = 0
    for i, chunk in enumerate(chunks):
        rows = 0
        for k in chunk:
            u_all[i % 2, rows : rows + u_refs[k].shape[0]] = u_refs[k][...]
            rows += u_refs[k].shape[0]
        s_all[i % 2, :rows] = dot(u_all[i % 2, :rows], v, NT)
        part = pair_elementwise(
            s_all.at[i % 2], g_ref.at[pl.ds(at, rows)], rows, scale2, bias2,
            at_ref[0, 0] if own and i == 0 else None,
        )
        tot = part if tot is None else tuple(a + b for a, b in zip(tot, part))
        du = dot(g_ref[at : at + rows], v, NN)
        at += rows
        rows = 0
        for k in chunk:
            ref = du_refs[k]
            ref[...] = du[rows : rows + ref.shape[0]].astype(ref.dtype)
            rows += ref.shape[0]
    for i in range(3):
        sums_ref[i] = tot[i] if own else tot[i] + before_ref[i]


def pair(chunks, own, scal, at, v, us, before=()):
    rows = sum(u.shape[0] for u in us)
    most = max(sum(us[k].shape[0] for k in c) for c in chunks)
    cols = v.shape[0]
    out = (
        *(jax.ShapeDtypeStruct(u.shape, BF16) for u in us),
        jax.ShapeDtypeStruct((rows, cols), BF16),
        jax.ShapeDtypeStruct((3, SUB, CB), F32),
    )
    return vmem_call(
        functools.partial(pair_kernel, chunks, own), out,
        scratch=(pltpu.VMEM((2, most, E), BF16), pltpu.VMEM((2, most, cols), F32)),
        specs=[SM, SM] + [VM] * (1 + len(before) + len(us)), out_specs=(VP,) * (len(us) + 2),
        flops=4 * rows * cols * E, nbytes=4 * (rows + cols) * E,
    )(scal, at, v, *before, *us)


def cols_kernel(n, *refs):
    g_refs, u_refs, (dv_hbm, done_ref, u_all, dv_ref, sem) = refs[:n], refs[n:-5], refs[-5:]
    done_ref[...] = jnp.zeros(done_ref.shape, F32)
    at = 0
    for ref in u_refs:
        u_all[at : at + R] = ref[...]
        at += R
    cols = dv_ref.shape[0] // 2
    put = []
    for i in range(2):
        at = pl.ds(i * cols, cols)
        dv = None
        row = 0
        for g in g_refs:
            k = g.shape[0]
            part = dot(g[:, at], u_all[row : row + k], TN)
            dv = part if dv is None else dv + part
            row += k
        dv_ref[at] = dv.astype(BF16)
        put.append(pltpu.make_async_copy(dv_ref.at[at], dv_hbm.at[at], sem.at[i]))
        put[i].start()
    for c in put:
        c.wait()


def pair_cols(gs, us):
    rows = sum(g.shape[0] for g in gs)
    cols = gs[0].shape[1]
    return vmem_call(
        functools.partial(cols_kernel, len(gs)),
        (jax.ShapeDtypeStruct((cols, E), BF16), jax.ShapeDtypeStruct((8, 128), F32)),
        scratch=(pltpu.VMEM((rows, E), BF16), pltpu.VMEM((cols, E), BF16), pltpu.SemaphoreType.DMA((2,))),
        specs=[VP] * len(gs) + [VM] * len(us), out_specs=(HB, VM),
        flops=2 * rows * cols * E, nbytes=2 * (rows * cols + rows * E + cols * E),
    )(*gs, *us)


def step_kernel(n, *refs):
    for k in range(n):
        refs[-n + k][...] = (refs[k][...].astype(F32) + refs[n + k][...].astype(F32)).astype(BF16)


STEP_FLOPS = 8 * 10**9


def ring_step(own, got, after=()):
    n = len(own)
    return vmem_call(
        functools.partial(step_kernel, n), (jax.ShapeDtypeStruct((R, E), BF16),) * n,
        specs=[VP] * n + [VM] * (n + len(after)), flops=STEP_FLOPS, nbytes=12 * R * E,
    )(*own, *got, *after)


def back_kernel(
    scal_ref, ui_hbm, ni_hbm, ut_hbm, nt_hbm, dv_hbm, du_ref, qa_ref, qb_ref,
    di_ref, dt_ref, keep_ref, send_ref, ui_ref, ni_ref, ut_ref, nt_ref, dv_ref, sem,
):
    get = [
        pltpu.make_async_copy(src, dst, sem.at[k])
        for k, (src, dst) in enumerate(
            ((ui_hbm, ui_ref), (ni_hbm, ni_ref), (ut_hbm, ut_ref), (nt_hbm, nt_ref), (dv_hbm, dv_ref))
        )
    ]
    for c in get:
        c.start()
    scale = scal_ref[0, 0]
    low = scal_ref[0, 1] == 0.0

    def finish(k, unit_ref, norm_ref, grad, out_ref):
        unit = unit_ref[...]
        d = (grad - unit * jnp.sum(unit * grad, axis=1, keepdims=True)) / norm_ref[:, :1]
        out_ref[...] = d.astype(BF16)
        left, right = d[:, :H], d[:, H:]
        keep_ref[k * R : (k + 1) * R] = jnp.where(low, left, right).astype(BF16)
        send_ref[k * R : (k + 1) * R] = jnp.where(low, right, left).astype(BF16)

    du = scale * (du_ref[...].astype(F32) + qa_ref[...].astype(F32) + qb_ref[...].astype(F32))
    get[0].wait()
    get[1].wait()
    finish(0, ui_ref, ni_ref, du, di_ref)
    for c in get[2:]:
        c.wait()
    dv = dv_ref[:R].astype(F32)
    for j in range(1, 8):
        dv = dv + dv_ref[j * R : (j + 1) * R].astype(F32)
    finish(1, ut_ref, nt_ref, scale * dv, dt_ref)


def back(scal, *args):
    low = jax.ShapeDtypeStruct((R, E), BF16)
    half = jax.ShapeDtypeStruct((2 * R, H), BF16)
    return vmem_call(
        back_kernel, (low, low, half, half), specs=[SM] + [HB] * 5 + [VP] + [VM] * 2,
        scratch=(
            pltpu.VMEM((R, E), F32),
            pltpu.VMEM((R, 128), F32),
            pltpu.VMEM((R, E), F32),
            pltpu.VMEM((R, 128), F32),
            pltpu.VMEM((8 * R, E), BF16),
            pltpu.SemaphoreType.DMA((5,)),
        ),
        flops=20 * R * E, nbytes=30 * R * E,
    )(scal, *args)


def input_grad_kernel(di_ref, dt_ref, head_ref, gi_ref, gt_ref, done_ref):
    head = head_ref[...]
    done_ref[...] = jnp.zeros((8, 128), F32)
    gi_ref[...] = dot(di_ref[...], head, NT).astype(BF16)
    gt_ref[...] = dot(dt_ref[...], head, NT).astype(BF16)


def input_grad(di, dt, head):
    out = jax.ShapeDtypeStruct((R, D), BF16)
    return vmem_call(
        input_grad_kernel, (out, out, jax.ShapeDtypeStruct((8, 128), F32)), n_in=3, flops=4 * R * D * E, nbytes=2 * (4 * R * D + D * E)
    )(di, dt, head)


ZROWS = 24
PAD = 16


def turn_kernel(*refs):
    hbm, (out_ref, x_all, sem) = refs[:4], refs[-3:]
    get = []
    for i, src in enumerate(hbm):
        get.append(pltpu.make_async_copy(src, x_all.at[pl.ds(i * R, R)], sem.at[i]))
        get[i].start()
    for c in get:
        c.wait()
    out_ref[...] = x_all[...].T


def turn(*data):
    return vmem_call(
        turn_kernel, jax.ShapeDtypeStruct((D, 4 * R), BF16),
        scratch=(pltpu.VMEM((4 * R, D), BF16), pltpu.SemaphoreType.DMA((4,))),
        specs=[HB] * 4, out_specs=VP, flops=4 * R * D, nbytes=16 * R * D,
    )(*data)


def own_head_kernel(xt_ref, keep_ref, out_ref):
    out_ref[...] = dot(xt_ref[:, : 2 * R], keep_ref[...], NN)


def own_head(xt, keep):
    return vmem_call(
        own_head_kernel, jax.ShapeDtypeStruct((D, H), F32), specs=[VP, VM], out_specs=VP,
        flops=4 * R * D * H, nbytes=4 * R * D + 4 * D * H,
    )(xt, keep)


def head_grad_kernel(xt_ref, own_ref, got_ref, extra_ref, out_hbm, out_v, out_sem):
    for j in range(8):
        out_v[j, 8 * ZROWS :] = extra_ref[...]
    d = got_ref[...]
    put = []
    for xl in range(2):
        rows = slice(xl * E, (xl + 1) * E)
        full = own_ref[rows] + dot(xt_ref[rows, 2 * R :], d, NN)
        for y in range(4):
            for z in range(0, 8, 2):
                a = (z * 4 + y) * ZROWS
                b = ((z + 1) * 4 + y) * ZROWS
                both = jnp.concatenate([full[a : a + ZROWS], full[b : b + ZROWS]], axis=0)
                out_v[xl * 4 + y, z * ZROWS : (z + 2) * ZROWS] = both.astype(BF16)
        at = pl.ds(xl * 4, 4)
        put.append(pltpu.make_async_copy(out_v.at[at], out_hbm.at[at], out_sem.at[xl]))
        put[xl].start()
    for c in put:
        c.wait()


def head_grad_parts(xt, own, got, extra):
    shape = (8, 8 * ZROWS + PAD, H)
    return vmem_call(
        head_grad_kernel, jax.ShapeDtypeStruct(shape, BF16),
        scratch=(pltpu.VMEM(shape, BF16), pltpu.SemaphoreType.DMA((2,))),
        specs=[VP, VP, VM, VM], out_specs=HB, flops=4 * R * D * H, nbytes=2 * (4 * R * D + D * H),
    )(xt, own, got, extra)


def sum_kernel(parts_hbm, _, out_ref, parts_v, sem):
    get = [pltpu.make_async_copy(parts_hbm.at[j], parts_v.at[j], sem.at[j]) for j in range(8)]
    for c in get:
        c.start()
    s = None
    for j in range(0, 8, 2):
        get[j].wait()
        get[j + 1].wait()
        pair_sum = parts_v[j].astype(F32) + parts_v[j + 1].astype(F32)
        s = pair_sum if s is None else s + pair_sum
    t = jnp.sum(s[8 * ZROWS : 8 * ZROWS + 3], axis=0, keepdims=True)
    hi = t.astype(BF16).astype(F32)
    mid = (t - hi).astype(BF16).astype(F32)
    low = t - hi - mid
    row = lax.broadcasted_iota(jnp.int32, (8, H), 0)
    tail = jnp.where(row == 0, hi, jnp.where(row == 1, mid, jnp.where(row == 2, low, 0.0)))
    for z in range(8):
        out_ref[z] = jnp.concatenate([s[z * ZROWS : (z + 1) * ZROWS], tail], axis=0).astype(BF16)


def sum_parts(parts, after):
    return vmem_call(
        sum_kernel, jax.ShapeDtypeStruct((8, ZROWS + 8, H), BF16), specs=[HB, VM],
        scratch=(pltpu.VMEM(parts.shape, BF16), pltpu.SemaphoreType.DMA((8,))),
        flops=10 * parts.size, nbytes=2 * parts.size,
    )(parts, after)


def last_kernel(scal_ref, s_ref, r_ref, o_ref, hg_ref, l_ref, a_ref, b_ref):
    low = scal_ref[0, 1] == 0.0
    mine = s_ref[...] + r_ref[...]
    other = o_ref[...]
    left = jnp.where(low, mine, other)
    right = jnp.where(low, other, mine)
    hg_ref[:, :H] = left[:ZROWS]
    hg_ref[:, H:] = right[:ZROWS]
    t = jnp.sum((mine + other)[ZROWS : ZROWS + 3], axis=0, keepdims=True) * (1.0 / COUNT)
    l_ref[...] = t[:, 0:1]
    a_ref[...] = scal_ref[0, 0] * t[:, 1:2]
    b_ref[...] = t[:, 2:3]


COUNT = float(4 * 8192) * 8192.0


def last(scal, s, r, o):
    one = jax.ShapeDtypeStruct((1, 1), F32)
    return vmem_call(
        last_kernel, (jax.ShapeDtypeStruct((ZROWS, E), F32), one, one, one), smem=1, n_in=4,
        flops=ZROWS * E, nbytes=16 * ZROWS * E,
    )(scal, s, r, o)


def swap(axis):
    return lambda v: lax.ppermute(v, axis, [(0, 1), (1, 0)])


def ring(axis, n):
    even = [(i, i ^ 1) for i in range(n)]
    odd = [(i, (i + 1) % n if i % 2 else (i - 1) % n) for i in range(n)]
    return (lambda v: lax.ppermute(v, axis, even)), (lambda v: lax.ppermute(v, axis, odd))


def split3(t):
    hi = lax.reduce_precision(t, 8, 7)
    mid = lax.reduce_precision(t - hi, 8, 7)
    return hi, mid, t - hi - mid


def scalar_rows(t, rows):
    parts = jnp.stack(split3(t))
    return jnp.concatenate([parts, jnp.zeros((rows - 3, H), F32)]).astype(BF16)


def per_device(image, text, log_scale, bias, head):
    x = image[0]
    y = text[0]
    scale = jnp.exp(log_scale)
    core = lax.axis_index("c")
    z1, z2 = ring("z", 8)
    cc = swap("c")
    near = ("xl", "y")

    u, v, ui, ni, ut, nt = project(x, y, head)

    a1, b1 = z1(u), z2(u)
    vs = lax.all_to_all(v, near, 0, 0, tiled=True)
    a2, b2 = z1(b1), z2(a1)
    a3, b3 = z1(b2), z2(a2)
    far = z1(b3)
    xt = turn(x, y, cc(x), cc(y))

    scal = jnp.stack([scale * LOG2E, bias * LOG2E]).reshape(1, 2)
    at = (lax.axis_index(near) * R).reshape(1, 1)
    us = (u, a1, b1, a2, b2, a3, b3)
    p0, pa1, pb1, pa2, pb2, g1, sums = pair(((0, 1), (2, 3, 4)), True, scal, at, vs, us[:5])
    pa3, pb3, g2, sums = pair(((0, 1),), False, scal, at, vs, us[5:], (sums,))
    pf, g3, sums = pair(((0,),), False, scal, at, vs, (far,), (sums,))

    dv, done = pair_cols((g1, g2, g3), (*us, far))
    (qa,) = ring_step((pb3,), (z1(pf),), (done,))
    dv = lax.all_to_all(dv, near, 0, 0, tiled=True)
    qa, qb = ring_step((pa2, pb2), (z2(qa), z1(pa3)))
    qa, qb = ring_step((pb1, pa1), (z1(qa), z2(qb)))
    qa, qb = z2(qa), z1(qb)

    sums = jnp.sum(sums, axis=(1, 2))
    extra = scalar_rows(jnp.zeros((H,), F32).at[:3].set(sums), PAD)

    scal2 = jnp.stack([scale, core.astype(F32)]).reshape(1, 2)
    di, dt, keep, send = back(scal2, ui, ni, ut, nt, dv, p0, qa, qb)
    got = cc(send)
    gi, gt, done = input_grad(di, dt, head)

    parts = head_grad_parts(xt, own_head(xt, keep), got, extra)
    parts = lax.all_to_all(parts, ("xl", "y"), 0, 0, tiled=True)
    parts = lax.all_to_all(sum_parts(parts, done), "z", 0, 0, tiled=True)
    s = jnp.sum(parts.astype(F32), axis=0)
    r = swap("xh")(s)
    o = cc(s + r)
    hg, l, a, b = last(scal2, s, r, o)
    return l.reshape(()), a.reshape(()), b.reshape(()), gi[None], gt[None], hg


def solution(mesh):
    fine = Mesh(mesh.devices.reshape(2, 8, 4, 2, 2), ("xl", "z", "y", "xh", "c"))
    blk = ("xl", "z", "y")
    rep = ("xh", "c")
    data = P(rep, blk, None)
    return jax.shard_map(
        per_device,
        mesh=fine,
        in_specs=(data, data, P(), P(), P()),
        out_specs=(P(), P(), P(), data, data, P(blk, None)),
        check_vma=False,
    )
```
